256 devices in a mesh: lon: 32 (over z, x), lat: 2 (over core), head: 4 (over y).
Axes of the slice: x: 4, y: 4, z: 8, core: 2. Of those that a mesh axis runs over, the one named last changes fastest.
Arguments:
- queries: bfloat16 [32, 1280, 1024], P('lat', 'lon', 'head'), may hold values from -49 to 49
- keys: bfloat16 [32, 1280, 1024], P('lat', 'lon', 'head'), may hold values from -49 to 49
- values: bfloat16 [32, 1280, 1024], P('lat', 'lon', 'head'), may hold values from -16 to 16
- grad_out: bfloat16 [32, 1280, 1024], P('lat', 'lon', 'head'), may hold values from -64 to 64
- key_mask: int32 [32, 1280], P('lat', 'lon'), may hold values from 0 to 1
- offsets: int32 [4, 160], P('lat', 'lon'), may hold values from -8 to 8, as said below
- regions: int32 [4, 160], P('lat', 'lon'), may hold values from 0 to 7
Outputs:
- grad_queries: bfloat16 [32, 1280, 1024], P('lat', 'lon', 'head')
- grad_keys: bfloat16 [32, 1280, 1024], P('lat', 'lon', 'head')
- grad_values: bfloat16 [32, 1280, 1024], P('lat', 'lon', 'head')
The draws below stay inside these ranges and needn't reach their ends.
Inputs may be any that keep to these rules, and one draw needn't show every extreme that they name: `offsets`: some block has offset -8 and some block has offset 8.
All inputs are finite; a program needn't handle non-finite values.
Results may differ from the reference program's by a relative error of at most 0.0095.
Values may be sent and summed in bfloat16 or wider, within the bound.
A program may use at most 64 MiB of HBM per device.

```python
import jax
import jax.numpy as jnp
from jax import lax

HEADS = 16
HS = 64
HD = 1024
WIN = 8
REG_DEV = 8
LAT_DEV = 16
LON_DEV = 40
NLAT = 32
NLON = 1280
NBLAT = 4
NBLON = 160
N_LON = 32
N_LAT = 2


def block_field(key):
    drawn = jnp.clip(jax.random.normal(key, (NBLAT, NBLON, HD), jnp.float32), -4.0, 4.0)
    return jnp.repeat(jnp.repeat(drawn, WIN, axis=0), WIN, axis=1)


def query_key_pair(key):
    noise_keys = jnp.clip(jax.random.normal(jax.random.fold_in(key, 11), (NLAT, NLON, HD), jnp.float32), -6.0, 6.0)
    base_keys = block_field(jax.random.fold_in(key, 16)) + 0.8 * noise_keys
    queries_drawn = jnp.clip(jax.random.normal(jax.random.fold_in(key, 12), (NLAT, NLON, HD), jnp.float32), -6.0, 6.0)
    keys_drawn = base_keys
    return (queries_drawn, keys_drawn)


def draw_queries(key, part):
    return query_key_pair(key)[0].astype(jnp.bfloat16)


def draw_keys(key, part):
    return query_key_pair(key)[1].astype(jnp.bfloat16)


def draw_values(key, part):
    common = block_field(jax.random.fold_in(key, 21))
    noise = jnp.clip(jax.random.normal(jax.random.fold_in(key, 22), (NLAT, NLON, HD), jnp.float32), -6.0, 6.0)
    drawn = common + 0.8 * noise
    return drawn.astype(jnp.bfloat16)


def draw_grad_out(key, part):
    row_common = jnp.clip(jax.random.normal(jax.random.fold_in(key, 31), (NBLAT, HD), jnp.float32), -4.0, 4.0)
    row_common = jnp.repeat(row_common, WIN, axis=0)[:, None, :]
    channel_mean = jnp.clip(jax.random.normal(jax.random.fold_in(key, 32), (HD,), jnp.float32), -4.0, 4.0)
    lat_frac = jnp.arange(NLAT, dtype=jnp.float32) / (NLAT - 1)
    noise = 0.8 * jnp.clip(jax.random.normal(jax.random.fold_in(key, 33), (NLAT, NLON, HD), jnp.float32), -6.0, 6.0)
    lat_scale = jnp.exp(lat_frac * 1.0986)
    drawn = (noise + row_common + 0.7 * channel_mean[None, None, :]) * lat_scale[:, None, None]
    return drawn.astype(jnp.bfloat16)


def draw_key_mask(key, part):
    lat_row = jnp.arange(NLAT, dtype=jnp.int32)
    distance = jnp.abs(2 * lat_row - (NLAT - 1))
    threshold = 950 - 700 * distance // NLAT
    ticket = jax.random.randint(key, (NLAT, NLON), 0, 1000)
    return (ticket < threshold[:, None]).astype(jnp.int32)


def draw_offsets(key, part):
    drawn = jax.random.randint(jax.random.fold_in(key, 1), (NBLAT, NBLON), -WIN, WIN + 1)
    west_row = jax.random.randint(jax.random.fold_in(key, 2), (), 0, NBLAT)
    east_row = jax.random.randint(jax.random.fold_in(key, 3), (), 0, NBLAT)
    drawn = drawn.at[west_row, 0].set(-WIN)
    drawn = drawn.at[east_row, NBLON - 1].set(WIN)
    return drawn.astype(jnp.int32)


def set_ends(entries, own_key, low, high):
    longest = entries.shape.index(max(entries.shape))
    spots = []
    for shift in (0, 1):
        where = [jax.random.randint(jax.random.fold_in(own_key, axis), (), 0, length) for axis, length in enumerate(entries.shape)]
        where[longest] = (where[longest] + shift) % entries.shape[longest]
        spots.append(tuple(where))
    return entries.at[spots[0]].set(low).at[spots[1]].set(high)


def setup_inputs(seed: int = 0) -> dict:
    key_of = jax.random.split(jax.random.key(seed), 8)
    queries = draw_queries(jax.random.fold_in(key_of[7], 71), 0)
    keys = draw_keys(jax.random.fold_in(key_of[7], 71), 0)
    values = draw_values(jax.random.fold_in(key_of[7], 71), 0)
    grad_out = draw_grad_out(jax.random.fold_in(key_of[7], 71), 0)
    key_mask = draw_key_mask(jax.random.fold_in(key_of[7], 71), 0)
    offsets = draw_offsets(jax.random.fold_in(key_of[7], 71), 0)
    regions = set_ends(jax.random.randint(key_of[6], (NBLAT, NBLON), 0, REG_DEV), jax.random.fold_in(key_of[6], 1), 0, REG_DEV - 1).astype(jnp.int32)
    return {"queries": queries, "keys": keys, "values": values, "grad_out": grad_out, "key_mask": key_mask, "offsets": offsets, "regions": regions}


MASKED_SCORE = -1.0e30


def round_low(array):
    return lax.optimization_barrier(array.astype(jnp.bfloat16)).astype(jnp.float32)


def to_blocks(array):
    lat_cells, lon_cells = array.shape[0], array.shape[1]
    trailing = array.shape[2:]
    grid_blocks = array.reshape((lat_cells // WIN, WIN, lon_cells // WIN, WIN) + trailing)
    perm_axes = (0, 2, 1, 3) + tuple(range(4, grid_blocks.ndim))
    return grid_blocks.transpose(perm_axes).reshape((lat_cells // WIN, lon_cells // WIN, WIN * WIN) + trailing)


def from_blocks(array):
    lat_blocks, lon_blocks = array.shape[0], array.shape[1]
    trailing = array.shape[3:]
    grid_blocks = array.reshape((lat_blocks, lon_blocks, WIN, WIN) + trailing)
    perm_axes = (0, 2, 1, 3) + tuple(range(4, grid_blocks.ndim))
    return grid_blocks.transpose(perm_axes).reshape((lat_blocks * WIN, lon_blocks * WIN) + trailing)


def window_of(array):
    lat_cells, lon_cells = array.shape[0], array.shape[1]
    trailing = array.shape[2:]
    grid_blocks = array.reshape((lat_cells // WIN, WIN, lon_cells // WIN, WIN) + trailing)
    stacked = jnp.stack([jnp.roll(grid_blocks, 2 - block_step, axis=2) for block_step in range(5)], axis=2)
    perm_axes = (0, 3, 2, 1, 4) + tuple(range(5, stacked.ndim))
    return stacked.transpose(perm_axes).reshape((lat_cells // WIN, lon_cells // WIN, 5 * WIN * WIN) + trailing)


def fold_back(grads):
    lat_blocks, lon_blocks = grads.shape[0], grads.shape[1]
    grid_blocks = grads.reshape(lat_blocks, lon_blocks, 5, WIN, WIN, grads.shape[-1])
    folded = jnp.roll(grid_blocks[:, :, 0], -2, axis=1)
    for block_step in range(1, 5):
        folded = folded + jnp.roll(grid_blocks[:, :, block_step], block_step - 2, axis=1)
    return from_blocks(folded.reshape(lat_blocks, lon_blocks, WIN * WIN, grads.shape[-1]))


def reference(queries, keys, values, grad_out, key_mask, offsets, regions):
    precise = lax.Precision.HIGHEST
    logit_scale = HS ** -0.5
    per_tile = LON_DEV // WIN
    reg_count = REG_DEV * N_LAT
    cell_region = jnp.repeat(jnp.repeat(regions, WIN, axis=0), WIN, axis=1)
    weights = (cell_region[:, :, None] == jnp.arange(REG_DEV, dtype=jnp.int32)[None, None, :]).astype(jnp.float32)
    weights = weights * key_mask.astype(jnp.float32)[:, :, None]
    weights = weights.reshape(N_LAT, LAT_DEV, N_LON, LON_DEV, REG_DEV)
    divisor = jnp.maximum(jnp.sum(weights, axis=(1, 3)), 1.0)

    def pool_tile(array):
        tiled = array.astype(jnp.float32).reshape(N_LAT, LAT_DEV, N_LON, LON_DEV, HD)
        sums = jnp.einsum("iajbr,iajbd->ijrd", weights, tiled, precision=precise)
        pooled = round_low(sums / divisor[:, :, :, None])
        return pooled.transpose(1, 0, 2, 3).reshape(N_LON, reg_count, HD)

    reg_key_all = jnp.repeat(pool_tile(keys), per_tile, axis=0)
    reg_val_all = jnp.repeat(pool_tile(values), per_tile, axis=0)

    key_offset = (jnp.arange(5, dtype=jnp.int32)[:, None, None] * WIN - 2 * WIN
                  + jnp.zeros((1, WIN, 1), jnp.int32)
                  + jnp.arange(WIN, dtype=jnp.int32)[None, None, :]).reshape(5 * WIN * WIN)
    window_start = offsets[:, :, None]
    mask_window = window_of(key_mask[:, :, None])[..., 0]
    usable = (key_offset >= window_start - WIN) & (key_offset < window_start + 2 * WIN) & (mask_window == 1)
    usable_b = usable[:, :, None, :]

    def one_head(head_index):
        def head_slice(array):
            return lax.dynamic_slice_in_dim(array, head_index * HS, HS, axis=2).astype(jnp.float32)

        query_block = to_blocks(head_slice(queries))
        gradient_block = to_blocks(head_slice(grad_out))
        cand_k = window_of(head_slice(keys))
        candidate_values = window_of(head_slice(values))
        register_key_rows = lax.dynamic_slice_in_dim(reg_key_all, head_index * HS, HS, axis=2)
        register_value_rows = lax.dynamic_slice_in_dim(reg_val_all, head_index * HS, HS, axis=2)
        score_win = jnp.einsum("abqd,abkd->abqk", query_block, cand_k) * logit_scale
        score_win = jnp.where(usable_b, score_win, MASKED_SCORE)
        register_scores = jnp.einsum("gstc,sfc->gstf", query_block, register_key_rows) * logit_scale
        row_max = jnp.maximum(jnp.max(score_win, axis=-1), jnp.max(register_scores, axis=-1))
        exp_total = jnp.sum(jnp.where(usable_b, jnp.exp(score_win - row_max[..., None]), 0.0), axis=-1)
        exp_total = exp_total + jnp.sum(jnp.exp(register_scores - row_max[..., None]), axis=-1)
        log_total = row_max + jnp.log(exp_total)
        prob_win = jnp.where(usable_b, jnp.exp(score_win - log_total[..., None]), 0.0)
        prob_reg = jnp.exp(register_scores - log_total[..., None])
        window_lower_bound = round_low(prob_win)
        register_lower_bound = round_low(prob_reg)
        attended_output = jnp.einsum("mzju,mzul->mzjl", window_lower_bound, candidate_values) + jnp.einsum("jpzf,pfm->jpzm", register_lower_bound, register_value_rows)
        delta_dot = jnp.sum(gradient_block * attended_output, axis=-1)
        dprob_win = jnp.einsum("abqd,abkd->abqk", gradient_block, candidate_values)
        register_prob_gradient = jnp.einsum("gstc,sfc->gstf", gradient_block, register_value_rows)
        dscore_win = round_low(prob_win * (dprob_win - delta_dot[..., None]))
        register_score_gradient = round_low(prob_reg * (register_prob_gradient - delta_dot[..., None]))
        grad_q = logit_scale * (jnp.einsum("mzju,mzul->mzjl", dscore_win, cand_k)
                                + jnp.einsum("jpzf,pfm->jpzm", register_score_gradient, register_key_rows))
        grad_kc = logit_scale * jnp.einsum("abqk,abqd->abkd", dscore_win, query_block)
        grad_vc = jnp.einsum("abqk,abqd->abkd", window_lower_bound, gradient_block)
        register_key_gradient = logit_scale * jnp.einsum("mcjz,mcjn->czn", register_score_gradient, query_block)
        register_value_gradient = jnp.einsum("mcjz,mcjn->czn", register_lower_bound, gradient_block)
        register_key_gradient = register_key_gradient.reshape(N_LON, per_tile, reg_count, HS).sum(axis=1)
        register_value_gradient = register_value_gradient.reshape(N_LON, per_tile, reg_count, HS).sum(axis=1)
        return from_blocks(grad_q), fold_back(grad_kc), fold_back(grad_vc), register_key_gradient, register_value_gradient

    head_ids = jnp.arange(HEADS, dtype=jnp.int32)
    grad_q, win_k, win_v, register_key_gradient, register_value_gradient = lax.map(one_head, head_ids)

    def merge_heads(array):
        return array.transpose(1, 2, 0, 3).reshape(array.shape[1], array.shape[2], HD)

    def to_cells(grad_reg):
        joined = merge_heads(grad_reg).reshape(N_LON, N_LAT, REG_DEV, HD).transpose(1, 0, 2, 3)
        scaled = joined / divisor[:, :, :, None]
        return jnp.einsum("iajbr,ijrd->iajbd", weights, scaled, precision=precise).reshape(NLAT, NLON, HD)

    grad_queries = merge_heads(grad_q).astype(jnp.bfloat16)
    grad_keys = (merge_heads(win_k) + to_cells(register_key_gradient)).astype(jnp.bfloat16)
    grad_values = (merge_heads(win_v) + to_cells(register_value_gradient)).astype(jnp.bfloat16)
    return grad_queries, grad_keys, grad_values
```

```python
import jax
import jax.numpy as jnp
from jax import lax
from jax.experimental import pallas as pl
from jax.experimental.pallas import tpu as pltpu
from jax.sharding import PartitionSpec as P

HS = 64
WIN = 8
CELLS = WIN * WIN
REG_DEV = 8
NA = 2
NB = 5
MASKED = -1.0e30
FLOOR = -1.0e29
SCALE = HS ** (-0.5)
MESH = pl.DeviceIdType.MESH
NT = (((1,), (1,)), ((), ()))
TN = (((0,), (0,)), ((), ()))
F32 = jnp.float32
BF16 = jnp.bfloat16

EDGE = ((0, 0, 3), (1, 0, 4), (3, 1, 5), (4, 2, 5))
FOREIGN = ((0, 0, -2, 0, 1), (0, 1, -1, 0, 2), (1, 0, 5, 3, 5), (1, 1, 6, 4, 5))


def dot(a, b, dims=(((1,), (0,)), ((), ()))):
    return lax.dot_general(a, b, dims, preferred_element_type=F32)


def kernel(
    q_hbm, k_hbm, v_hbm, g_hbm, mask_hbm, off_hbm, reg_hbm,
    o_q, o_k, o_v,
    q_in, k_in, v_in, g_in, kb, vb, mrep,
    fq, fg, e_s, p_s, dk_s, dv_s, dq_s, rk_s, rv_s,
    pool, rsend, rrecv, st_out, st_in, pst_out, pst_in, dq_out, dq_in,
    mask_ref, off_ref, reg_ref,
    in_sem, qg_ss, qg_rs, st_ss, st_rs, pst_ss, pst_rs, dq_ss, dq_rs, lat_ss, lat_rs,
):
    count = lax.axis_size("lon")
    me = lax.axis_index("lon")
    right = lax.rem(me + 1, count)
    left = lax.rem(me + count - 1, count)
    peer = 1 - lax.axis_index("lat")
    sides = ({"lon": left}, {"lon": right})

    barrier = pltpu.get_barrier_semaphore()
    for device in sides + ({"lat": peer},):
        pl.semaphore_signal(barrier, inc=1, device_id=device, device_id_type=MESH)
    loads = [
        pltpu.make_async_copy(src, dst, in_sem.at[i])
        for i, (src, dst) in enumerate((
            (mask_hbm, mask_ref), (off_hbm, off_ref), (reg_hbm, reg_ref),
            (k_hbm, k_in), (v_hbm, v_in), (q_hbm, q_in), (g_hbm, g_in),
        ))
    ]
    for copy in loads:
        copy.start()
    pl.semaphore_wait(barrier, 3)

    def qg_copy(side, a, slot, kind):
        block = slot + (0 if side == 0 else 3)
        src = (q_hbm, g_hbm)[kind]
        dst = (fq, fg)[kind]
        return pltpu.make_async_remote_copy(
            src.at[a, :, block], dst.at[1 - side, a, slot],
            qg_ss.at[side, a, slot, kind], qg_rs.at[1 - side, a, slot, kind],
            device_id=sides[side], device_id_type=MESH,
        )

    for a in range(NA):
        for slot in range(2):
            for kind in range(2):
                for side in range(2):
                    qg_copy(side, a, slot, kind).start()

    def rows_copy(src, dst, ss, rs, side, a):
        return pltpu.make_async_remote_copy(
            src.at[side, a], dst.at[1 - side, a], ss.at[side, a], rs.at[1 - side, a],
            device_id=sides[side], device_id_type=MESH,
        )

    lane_head = lax.broadcasted_iota(jnp.int32, (CELLS, 4 * HS), 1) // HS
    head_mask = [(lane_head == h).astype(F32).astype(BF16) for h in range(4)]
    low_half = lax.broadcasted_iota(jnp.int32, (CELLS, 128), 1) < HS

    def block_diag(x):
        return jnp.concatenate([x * head_mask[h] for h in range(4)], axis=0)

    def diag_rows(full):
        return jnp.concatenate(
            [
                jnp.where(low_half, full[0:64, 0:128], full[64:128, 0:128]),
                jnp.where(low_half, full[128:192, 128:256], full[192:256, 128:256]),
            ],
            axis=1,
        )

    for copy in loads:
        copy.wait()

    cell_t = lax.broadcasted_iota(jnp.int32, (CELLS, NB * WIN), 0) % WIN
    lane = lax.broadcasted_iota(jnp.int32, (CELLS, NB * WIN), 1)
    row8 = lax.broadcasted_iota(jnp.int32, (REG_DEV, 256), 0)
    pk = jnp.zeros((REG_DEV, 256), F32)
    pv = jnp.zeros((REG_DEV, 256), F32)
    cnt = jnp.zeros((REG_DEV, 256), F32)
    for a in range(NA):
        mask8 = mask_ref[a * WIN : (a + 1) * WIN, :].astype(F32)
        mask64 = jnp.broadcast_to(mask8[:, None, :], (WIN, WIN, NB * WIN)).reshape(CELLS, NB * WIN)
        for b in range(NB):
            column = jnp.sum(jnp.where(lane == cell_t + b * WIN, mask64, 0.0), axis=1, keepdims=True)
            rep = jnp.broadcast_to(column, (CELLS, 128))
            mrep[a, b * CELLS : (b + 1) * CELLS, :] = rep
            rep2 = jnp.concatenate([rep, rep], axis=1)
            kx = k_in[a, :, b].reshape(CELLS, 256)
            vx = v_in[a, :, b].reshape(CELLS, 256)
            kb[a, b * CELLS : (b + 1) * CELLS, :] = kx
            vb[a, b * CELLS : (b + 1) * CELLS, :] = vx
            mine = row8 == reg_ref[a, b]
            pk = pk + jnp.where(mine, jnp.sum(kx.astype(F32) * rep2, axis=0, keepdims=True), 0.0)
            pv = pv + jnp.where(mine, jnp.sum(vx.astype(F32) * rep2, axis=0, keepdims=True), 0.0)
            cnt = cnt + jnp.where(mine, jnp.sum(rep2, axis=0, keepdims=True), 0.0)
    divisor = jnp.maximum(cnt, 1.0)
    pool[0, 0] = (pk / divisor).astype(BF16)
    pool[0, 1] = (pv / divisor).astype(BF16)
    pool_copy = pltpu.make_async_remote_copy(
        pool.at[0], pool.at[1], lat_ss.at[0], lat_rs.at[0], device_id={"lat": peer}, device_id_type=MESH
    )
    pool_copy.start()
    dk_s[...] = jnp.zeros_like(dk_s)
    dv_s[...] = jnp.zeros_like(dv_s)
    rk_s[...] = jnp.zeros_like(rk_s)
    rv_s[...] = jnp.zeros_like(rv_s)
    pool_copy.wait_recv()
    reg_k = jnp.concatenate([pool[0, 0].astype(F32), pool[1, 0].astype(F32)], axis=0).astype(BF16)
    reg_v = jnp.concatenate([pool[0, 1].astype(F32), pool[1, 1].astype(F32)], axis=0).astype(BF16)

    def bias(a, block, first, end, start):
        rows = (end - first) * CELLS
        row = lax.broadcasted_iota(jnp.int32, (rows, 128), 0)
        key_off = row // CELLS * WIN + row % WIN + (first - block) * WIN
        usable = (key_off >= start - WIN) & (key_off < start + 2 * WIN)
        usable = usable & (mrep[a, first * CELLS : end * CELLS, :] > 0.5)
        half = jnp.where(usable, 0.0, MASKED)
        return jnp.concatenate([half, half], axis=1)

    def partial_stats(keys, values, bdq, bdg, add):
        s = dot(keys, bdq, NT) + add
        dp = dot(values, bdg, NT)
        top = jnp.maximum(jnp.max(s, axis=0, keepdims=True), FLOOR)
        e = jnp.exp(s - top)
        total = jnp.sum(e, axis=0, keepdims=True)
        inner = jnp.sum(e * dp, axis=0, keepdims=True)
        return e, dp, (top, total, inner)

    def merged(x, y):
        top = jnp.maximum(x[0], y[0])
        fx = jnp.exp(x[0] - top)
        fy = jnp.exp(y[0] - top)
        inverse = 1.0 / (x[1] * fx + y[1] * fy)
        return fx * inverse, (x[2] * fx + y[2] * fy) * inverse

    def grads(a, first, end, keys, bdq, bdg, e, dp, alpha, delta, regs):
        rows = (end - first) * CELLS
        p = e * alpha
        ds = (p * (dp - delta)).astype(BF16)
        p = p.astype(BF16)
        dv = dot(p, bdg)
        dk = dot(ds, bdq)
        dv_s[a, first * CELLS : end * CELLS, :] += dv[:rows]
        dk_s[a, first * CELLS : end * CELLS, :] += dk[:rows]
        if regs:
            rv_s[...] += dv[rows:]
            rk_s[...] += dk[rows:]
        return diag_rows(dot(ds, keys, TN)) * SCALE

    def local_q(a, block):
        bdq = block_diag(q_in[a, :, block].reshape(CELLS, 256) * jnp.asarray(SCALE, BF16))
        bdg = block_diag(g_in[a, :, block].reshape(CELLS, 256))
        return bdq, bdg

    def local_keys(a, first, end):
        keys = jnp.concatenate([kb[a, first * CELLS : end * CELLS, :], reg_k], axis=0)
        values = jnp.concatenate([vb[a, first * CELLS : end * CELLS, :], reg_v], axis=0)
        return keys, values

    def local_stats(a, block, first, end):
        keys, values = local_keys(a, first, end)
        bdq, bdg = local_q(a, block)
        add = jnp.concatenate(
            [bias(a, block, first, end, off_ref[a, block]), jnp.zeros((2 * REG_DEV, 256), F32)], axis=0
        )
        e, dp, stats = partial_stats(keys, values, bdq, bdg, add)
        return keys, bdq, bdg, e, dp, stats

    def edge_stats(a, carry):
        for i, (block, first, end) in enumerate(EDGE):
            rows = (end - first) * CELLS + 2 * REG_DEV
            _, _, _, e, dp, stats = local_stats(a, block, first, end)
            e_s[a, i, :rows] = e
            p_s[a, i, :rows] = dp
            side, slot = i // 2, i % 2
            st_out[side, a, slot, 0:1] = stats[0]
            st_out[side, a, slot, 1:2] = stats[1]
            st_out[side, a, slot, 2:3] = stats[2]
            st_out[side, a, slot, 3:4] = jnp.full((1, 256), off_ref[a, block], jnp.int32).astype(F32)
        for side in range(2):
            rows_copy(st_out, st_in, st_ss, st_rs, side, a).start()
        return carry

    def middle(a, carry):
        keys, bdq, bdg, e, dp, stats = local_stats(a, 2, 0, NB)
        inverse = 1.0 / stats[1]
        dq = grads(a, 0, NB, keys, bdq, bdg, e, dp, inverse, stats[2] * inverse, True)
        o_q[a, :, 2] = dq.reshape(WIN, WIN, 256).astype(BF16)
        return carry

    def foreign(a, carry):
        for side in range(2):
            for slot in range(2):
                for kind in range(2):
                    qg_copy(1 - side, a, slot, kind).wait_recv()
            rows_copy(st_out, st_in, st_ss, st_rs, 1 - side, a).wait_recv()
        for side, slot, block, first, end in FOREIGN:
            keys = kb[a, first * CELLS : end * CELLS, :]
            values = vb[a, first * CELLS : end * CELLS, :]
            bdq = block_diag(fq[side, a, slot].reshape(CELLS, 256) * jnp.asarray(SCALE, BF16))
            bdg = block_diag(fg[side, a, slot].reshape(CELLS, 256))
            theirs = tuple(st_in[side, a, slot, r : r + 1] for r in range(3))
            start = st_in[side, a, slot, 3:4, 0:128].astype(jnp.int32)
            e, dp, stats = partial_stats(keys, values, bdq, bdg, bias(a, block, first, end, start))
            for r in range(3):
                pst_out[side, a, slot, r : r + 1] = stats[r]
            alpha, delta = merged(stats, theirs)
            dq = grads(a, first, end, keys, bdq, bdg, e, dp, alpha, delta, False)
            dq_out[side, a, slot] = dq.astype(BF16)
        for side in range(2):
            rows_copy(pst_out, pst_in, pst_ss, pst_rs, side, a).start()
            rows_copy(dq_out, dq_in, dq_ss, dq_rs, side, a).start()
        return carry

    def finish(a, carry):
        for side in range(2):
            rows_copy(pst_out, pst_in, pst_ss, pst_rs, 1 - side, a).wait_recv()
        for i, (block, first, end) in enumerate(EDGE):
            side, slot = i // 2, i % 2
            rows = (end - first) * CELLS + 2 * REG_DEV
            keys, _ = local_keys(a, first, end)
            bdq, bdg = local_q(a, block)
            mine = tuple(st_out[side, a, slot, r : r + 1] for r in range(3))
            theirs = tuple(pst_in[side, a, slot, r : r + 1] for r in range(3))
            alpha, delta = merged(mine, theirs)
            dq_s[a, i] = grads(
                a, first, end, keys, bdq, bdg, e_s[a, i, :rows], p_s[a, i, :rows], alpha, delta, True
            )
        return carry

    lax.fori_loop(0, NA, edge_stats, 0)
    lax.fori_loop(0, NA, middle, 0)
    lax.fori_loop(0, NA, foreign, 0)
    lax.fori_loop(0, NA, finish, 0)

    rsend[0] = rk_s[REG_DEV:, :]
    rsend[1] = rv_s[REG_DEV:, :]
    reg_copy = pltpu.make_async_remote_copy(
        rsend, rrecv, lat_ss.at[1], lat_rs.at[1], device_id={"lat": peer}, device_id_type=MESH
    )
    reg_copy.start()
    reg_copy.wait_recv()
    own_k = (rk_s[:REG_DEV, :] + rrecv[0]) / divisor
    own_v = (rv_s[:REG_DEV, :] + rrecv[1]) / divisor
    for a in range(NA):
        for b in range(NB):
            mine = row8 == reg_ref[a, b]
            rep = mrep[a, b * CELLS : (b + 1) * CELLS, :]
            rep2 = jnp.concatenate([rep, rep], axis=1)
            row_k = jnp.sum(jnp.where(mine, own_k, 0.0), axis=0, keepdims=True)
            row_v = jnp.sum(jnp.where(mine, own_v, 0.0), axis=0, keepdims=True)
            dk = dk_s[a, b * CELLS : (b + 1) * CELLS, :] + rep2 * row_k
            dv = dv_s[a, b * CELLS : (b + 1) * CELLS, :] + rep2 * row_v
            o_k[a, :, b] = dk.reshape(WIN, WIN, 256).astype(BF16)
            o_v[a, :, b] = dv.reshape(WIN, WIN, 256).astype(BF16)
    for a in range(NA):
        for side in range(2):
            rows_copy(dq_out, dq_in, dq_ss, dq_rs, 1 - side, a).wait_recv()
        for i, (block, _, _) in enumerate(EDGE):
            side, slot = i // 2, i % 2
            dq = dq_s[a, i] + dq_in[side, a, slot].astype(F32)
            o_q[a, :, block] = dq.reshape(WIN, WIN, 256).astype(BF16)
    for side in range(2):
        for a in range(NA):
            for slot in range(2):
                for kind in range(2):
                    qg_copy(side, a, slot, kind).wait_send()
            rows_copy(st_out, st_in, st_ss, st_rs, side, a).wait_send()
            rows_copy(pst_out, pst_in, pst_ss, pst_rs, side, a).wait_send()
            rows_copy(dq_out, dq_in, dq_ss, dq_rs, side, a).wait_send()
    pool_copy.wait_send()
    reg_copy.wait_send()


def store(a_in, b_in, c_in, a_out, b_out, c_out, sem):
    copies = [
        pltpu.make_async_copy(src, dst, sem.at[i])
        for i, (src, dst) in enumerate(((a_in, a_out), (b_in, b_out), (c_in, c_out)))
    ]
    for copy in copies:
        copy.start()
    for copy in copies:
        copy.wait()


def local(queries, keys, values, grad_out, key_mask, offsets, regions):
    shape = queries.shape
    grid = (NA, WIN, NB, WIN, 256)
    hbm_spec = pl.BlockSpec(memory_space=pltpu.HBM)
    vmem_spec = pl.BlockSpec(memory_space=pltpu.VMEM)
    vm = pltpu.VMEM
    dma = pltpu.SemaphoreType.DMA
    outs = pl.pallas_call(
        kernel,
        out_shape=[jax.ShapeDtypeStruct(grid, BF16)] * 3,
        in_specs=[hbm_spec] * 7,
        out_specs=[vmem_spec] * 3,
        scratch_shapes=[vm(grid, BF16)] * 4
        + [vm((NA, NB * CELLS, 256), BF16)] * 2
        + [vm((NA, NB * CELLS, 128), F32)]
        + [vm((2, NA, 2, WIN, WIN, 256), BF16)] * 2
        + [vm((NA, 4, 4 * CELLS + 2 * REG_DEV, 256), F32)] * 2
        + [vm((NA, NB * CELLS, 256), F32)] * 2
        + [vm((NA, 4, CELLS, 256), F32)]
        + [vm((2 * REG_DEV, 256), F32)] * 2
        + [vm((2, 2, REG_DEV, 256), BF16)]
        + [vm((2, REG_DEV, 256), F32)] * 2
        + [vm((2, NA, 2, 8, 256), F32)] * 4
        + [vm((2, NA, 2, CELLS, 256), BF16)] * 2
        + [vm(key_mask.shape, jnp.int32)]
        + [pltpu.SMEM(offsets.shape, jnp.int32)] * 2
        + [dma((7,))]
        + [dma((2, NA, 2, 2))] * 2
        + [dma((2, NA))] * 6
        + [dma((2,))] * 2,
        compiler_params=pltpu.CompilerParams(
            collective_id=0, has_side_effects=True, vmem_limit_bytes=67108864
        ),
        cost_estimate=pl.CostEstimate(flops=2200000000, bytes_accessed=2300000, transcendentals=860000),
    )(
        *(x.reshape(grid) for x in (queries, keys, values, grad_out)), key_mask, offsets, regions
    )
    return tuple(x.reshape(shape) for x in outs)


def solution(mesh):
    tile = P("lat", "lon", "head")
    cells = P("lat", "lon")
    return jax.shard_map(
        local, mesh=mesh, in_specs=(tile,) * 4 + (cells,) * 3, out_specs=(tile,) * 3, check_vma=False
    )
```

```python
import jax
import jax.numpy as jnp
from jax import lax
from jax.experimental import pallas as pl
from jax.experimental.pallas import tpu as pltpu
from jax.sharding import PartitionSpec as P

HS = 64
WIN = 8
CELLS = WIN * WIN
REG_DEV = 8
NA = 2
NB = 5
VMEM_BYTES = 64 * 1024 * 1024
MASKED = -1.0e30
FLOOR = -1.0e29
SCALE = HS ** (-0.5)
MESH = pl.DeviceIdType.MESH
NT = (((1,), (1,)), ((), ()))
TN = (((0,), (0,)), ((), ()))
F32 = jnp.float32
BF16 = jnp.bfloat16

EDGE = (
    (0, 0, 3, 0, 0, 2, -2), (1, 0, 4, 0, 1, 2, -1),
    (3, 1, 5, 1, 0, 1, 5), (4, 2, 5, 1, 0, 2, 5),
)
FOREIGN = (((0, -2, 0, 1), (1, -1, 0, 2)), ((0, 5, 3, 5), (1, 6, 4, 5)))


def dot(a, b, dims=(((1,), (0,)), ((), ()))):
    return lax.dot_general(a, b, dims, preferred_element_type=F32)


def kernel(
    q_hbm, k_hbm, v_hbm, g_hbm, mask_hbm, off_hbm, reg_hbm,
    oq_hbm, ok_hbm, ov_hbm,
    q_in, k_in, v_in, g_in, kb, vb, mrep, frep,
    fk, fv, fq, fg, fmask, e_s, p_s, dk_s, dv_s, rk_s, rv_s,
    pool, rsend, rrecv, st_out, st_in, o_q, o_k, o_v,
    mask_ref, off_ref, reg_ref,
    in_sem, out_sem, kv_ss, kv_rs, qg_ss, qg_rs, mk_ss, mk_rs, st_ss, st_rs, lat_ss, lat_rs, late,
):
    count = lax.axis_size("lon")
    me = lax.axis_index("lon")
    right = lax.rem(me + 1, count)
    left = lax.rem(me + count - 1, count)
    peer = 1 - lax.axis_index("lat")
    sides = ({"lon": left}, {"lon": right})
    first_tile = me == 0
    last_tile = me == count - 1

    barrier = pltpu.get_barrier_semaphore()
    for device in (sides[0], {"lat": peer}):
        pl.semaphore_signal(barrier, inc=1, device_id=device, device_id_type=MESH)

    @pl.when(jnp.logical_not(last_tile))
    def _():
        pl.semaphore_signal(barrier, inc=1, device_id=sides[1], device_id_type=MESH)

    loads = [
        pltpu.make_async_copy(src, dst, in_sem.at[i])
        for i, (src, dst) in enumerate((
            (mask_hbm, mask_ref), (off_hbm, off_ref), (reg_hbm, reg_ref),
            (k_hbm, k_in), (v_hbm, v_in), (q_hbm, q_in), (g_hbm, g_in),
        ))
    ]
    for copy in loads:
        copy.start()
    pl.semaphore_wait(barrier, jnp.where(first_tile, 2, 3))

    @pl.when(last_tile)
    def _():
        pl.semaphore_signal(late, inc=1, device_id=sides[1], device_id_type=MESH)

    def edge_blocks(side):
        return pl.ds(0 if side == 0 else 3, 2)

    def remote(src, dst, ss, rs, side):
        return pltpu.make_async_remote_copy(
            src, dst, ss, rs, device_id=sides[side], device_id_type=MESH
        )

    def mask_copy(side):
        return remote(mask_hbm, fmask.at[1 - side], mk_ss.at[side], mk_rs.at[1 - side], side)

    def kv_copy(side, kind):
        src = (k_hbm, v_hbm)[kind].at[:, :, edge_blocks(side)]
        dst = (fk, fv)[kind].at[1 - side]
        return remote(src, dst, kv_ss.at[side, kind], kv_rs.at[1 - side, kind], side)

    def qg_copy(side, a, kind):
        src = (q_hbm, g_hbm)[kind].at[a, :, edge_blocks(side)]
        dst = (fq, fg)[kind].at[1 - side, a]
        return remote(src, dst, qg_ss.at[side, a, kind], qg_rs.at[1 - side, a, kind], side)

    def st_copy(side):
        return remote(st_out.at[side], st_in.at[1 - side], st_ss.at[side], st_rs.at[1 - side], side)

    def bulk(side):
        copies = [mask_copy(side)] + [kv_copy(side, kind) for kind in range(2)]
        return copies + [qg_copy(side, a, kind) for a in range(NA) for kind in range(2)]

    for copy in bulk(1):
        copy.start()

    @pl.when(jnp.logical_not(first_tile))
    def _():
        for copy in bulk(0):
            copy.start()

    lane_head = lax.broadcasted_iota(jnp.int32, (CELLS, 4 * HS), 1) // HS
    head_mask = [(lane_head == h).astype(F32).astype(BF16) for h in range(4)]
    low_half = lax.broadcasted_iota(jnp.int32, (CELLS, 128), 1) < HS

    def block_diag(x):
        return jnp.concatenate([x * head_mask[h] for h in range(4)], axis=0)

    def diag_rows(full):
        return jnp.concatenate(
            [
                jnp.where(low_half, full[0:64, 0:128], full[64:128, 0:128]),
                jnp.where(low_half, full[128:192, 128:256], full[192:256, 128:256]),
            ],
            axis=1,
        )

    for copy in loads:
        copy.wait()

    cell_t = lax.broadcasted_iota(jnp.int32, (CELLS, NB * WIN), 0) % WIN
    lane = lax.broadcasted_iota(jnp.int32, (CELLS, NB * WIN), 1)
    row8 = lax.broadcasted_iota(jnp.int32, (REG_DEV, 256), 0)

    def mask_rows(mask8):
        mask8 = mask8.astype(F32)
        return jnp.broadcast_to(mask8[:, None, :], (WIN, WIN, NB * WIN)).reshape(CELLS, NB * WIN)

    def mask_cells(mask64, b):
        column = jnp.sum(jnp.where(lane == cell_t + b * WIN, mask64, 0.0), axis=1, keepdims=True)
        return jnp.broadcast_to(column, (CELLS, 128))

    pk = jnp.zeros((REG_DEV, 256), F32)
    pv = jnp.zeros((REG_DEV, 256), F32)
    cnt = jnp.zeros((REG_DEV, 256), F32)
    for a in range(NA):
        mask64 = mask_rows(mask_ref[a * WIN : (a + 1) * WIN, :])
        for b in range(NB):
            rep = mask_cells(mask64, b)
            mrep[a, b * CELLS : (b + 1) * CELLS, :] = rep
            rep2 = jnp.concatenate([rep, rep], axis=1)
            kx = k_in[a, :, b].reshape(CELLS, 256)
            vx = v_in[a, :, b].reshape(CELLS, 256)
            kb[a, b * CELLS : (b + 1) * CELLS, :] = kx
            vb[a, b * CELLS : (b + 1) * CELLS, :] = vx
            mine = row8 == reg_ref[a, b]
            pk = pk + jnp.where(mine, jnp.sum(kx.astype(F32) * rep2, axis=0, keepdims=True), 0.0)
            pv = pv + jnp.where(mine, jnp.sum(vx.astype(F32) * rep2, axis=0, keepdims=True), 0.0)
            cnt = cnt + jnp.where(mine, jnp.sum(rep2, axis=0, keepdims=True), 0.0)
    divisor = jnp.maximum(cnt, 1.0)
    pool[0, 0] = (pk / divisor).astype(BF16)
    pool[0, 1] = (pv / divisor).astype(BF16)
    pool_copy = pltpu.make_async_remote_copy(
        pool.at[0], pool.at[1], lat_ss.at[0], lat_rs.at[0], device_id={"lat": peer}, device_id_type=MESH
    )
    pool_copy.start()
    dk_s[...] = jnp.zeros_like(dk_s)
    dv_s[...] = jnp.zeros_like(dv_s)
    rk_s[...] = jnp.zeros_like(rk_s)
    rv_s[...] = jnp.zeros_like(rv_s)
    pool_copy.wait_recv()
    reg_k = jnp.concatenate([pool[0, 0].astype(F32), pool[1, 0].astype(F32)], axis=0).astype(BF16)
    reg_v = jnp.concatenate([pool[0, 1].astype(F32), pool[1, 1].astype(F32)], axis=0).astype(BF16)

    def bias(rep, relative, start):
        row = lax.broadcasted_iota(jnp.int32, rep.shape, 0)
        key_off = row // CELLS * WIN + row % WIN + relative * WIN
        usable = (key_off >= start - WIN) & (key_off < start + 2 * WIN) & (rep > 0.5)
        half = jnp.where(usable, 0.0, MASKED)
        return jnp.concatenate([half, half], axis=1)

    def partial_stats(keys, values, bdq, bdg, add):
        s = dot(keys, bdq, NT) + add
        dp = dot(values, bdg, NT)
        top = jnp.maximum(jnp.max(s, axis=0, keepdims=True), FLOOR)
        e = jnp.exp(s - top)
        total = jnp.sum(e, axis=0, keepdims=True)
        inner = jnp.sum(e * dp, axis=0, keepdims=True)
        return e, dp, (top, total, inner)

    def merged(x, y):
        top = jnp.maximum(x[0], y[0])
        fx = jnp.exp(x[0] - top)
        fy = jnp.exp(y[0] - top)
        inverse = 1.0 / (x[1] * fx + y[1] * fy)
        return fx * inverse, fy * inverse, (x[2] * fx + y[2] * fy) * inverse

    def weights(e, dp, alpha, delta):
        p = e * alpha
        ds = p * (dp - delta)
        return p.astype(BF16), ds.astype(BF16)

    def add_key_grads(a, first, end, p, ds, bdq, bdg, regs):
        rows = (end - first) * CELLS
        dv = dot(p, bdg)
        dk = dot(ds, bdq)
        dv_s[a, first * CELLS : end * CELLS, :] += dv[:rows]
        dk_s[a, first * CELLS : end * CELLS, :] += dk[:rows]
        if regs:
            rv_s[...] += dv[rows:]
            rk_s[...] += dk[rows:]

    def diag_pair(q, g):
        bdq = block_diag(q.reshape(CELLS, 256) * jnp.asarray(SCALE, BF16))
        return bdq, block_diag(g.reshape(CELLS, 256))

    def local_q(a, block):
        return diag_pair(q_in[a, :, block], g_in[a, :, block])

    def local_keys(a, first, end):
        keys = jnp.concatenate([kb[a, first * CELLS : end * CELLS, :], reg_k], axis=0)
        values = jnp.concatenate([vb[a, first * CELLS : end * CELLS, :], reg_v], axis=0)
        return keys, values

    def local_stats(a, block, first, end):
        keys, values = local_keys(a, first, end)
        bdq, bdg = local_q(a, block)
        rep = mrep[a, first * CELLS : end * CELLS, :]
        add = jnp.concatenate(
            [bias(rep, first - block, off_ref[a, block]), jnp.zeros((2 * REG_DEV, 256), F32)], axis=0
        )
        e, dp, stats = partial_stats(keys, values, bdq, bdg, add)
        return keys, bdq, bdg, e, dp, stats

    def edge_stats(a, carry):
        for i, (block, first, end, side, _, _, _) in enumerate(EDGE):
            rows = (end - first) * CELLS + 2 * REG_DEV
            _, _, _, e, dp, stats = local_stats(a, block, first, end)
            e_s[a, i, :rows] = e
            p_s[a, i, :rows] = dp
            slot = i % 2
            for r in range(3):
                st_out[side, a, slot, r : r + 1] = stats[r]
            st_out[side, a, slot, 3:4] = jnp.full((1, 256), off_ref[a, block], jnp.int32).astype(F32)
        return carry

    def middle(a, carry):
        keys, bdq, bdg, e, dp, stats = local_stats(a, 2, 0, NB)
        inverse = 1.0 / stats[1]
        p, ds = weights(e, dp, inverse, stats[2] * inverse)
        add_key_grads(a, 0, NB, p, ds, bdq, bdg, True)
        dq = diag_rows(dot(ds, keys, TN)) * SCALE
        o_q[a, :, 2] = dq.reshape(WIN, WIN, 256).astype(BF16)
        return carry

    def foreign_keys(side):
        mask_copy(1 - side).wait_recv()
        for kind in range(2):
            kv_copy(1 - side, kind).wait_recv()

        def body(a, carry):
            mask64 = mask_rows(fmask[side, pl.ds(pl.multiple_of(a * WIN, WIN), WIN), :])
            for slot in range(2):
                frep[slot * CELLS : (slot + 1) * CELLS, :] = mask_cells(mask64, slot + (3 if side == 0 else 0))
            for i, (block, first, end, edge_side, low, high, relative) in enumerate(EDGE):
                if edge_side != side:
                    continue
                rows = (end - first) * CELLS + 2 * REG_DEV
                far_k = jnp.concatenate(
                    [fk[side, a, :, slot].reshape(CELLS, 256) for slot in range(low, high)], axis=0
                )
                far_v = jnp.concatenate(
                    [fv[side, a, :, slot].reshape(CELLS, 256) for slot in range(low, high)], axis=0
                )
                keys, _ = local_keys(a, first, end)
                bdq, bdg = local_q(a, block)
                add = bias(frep[low * CELLS : high * CELLS, :], relative - block, off_ref[a, block])
                far_e, far_dp, far = partial_stats(far_k, far_v, bdq, bdg, add)
                near = tuple(st_out[side, a, i % 2, r : r + 1] for r in range(3))
                alpha, far_alpha, delta = merged(near, far)
                p, ds = weights(e_s[a, i, :rows], p_s[a, i, :rows], alpha, delta)
                _, far_ds = weights(far_e, far_dp, far_alpha, delta)
                dq = diag_rows(dot(ds, keys, TN) + dot(far_ds, far_k, TN)) * SCALE
                add_key_grads(a, first, end, p, ds, bdq, bdg, True)
                o_q[a, :, block] = dq.reshape(WIN, WIN, 256).astype(BF16)
            return carry

        lax.fori_loop(0, NA, body, 0)

    def foreign_queries(side):
        st_copy(1 - side).wait_recv()

        def body(a, carry):
            for kind in range(2):
                qg_copy(1 - side, a, kind).wait_recv()
            for slot, block, first, end in FOREIGN[side]:
                keys = kb[a, first * CELLS : end * CELLS, :]
                values = vb[a, first * CELLS : end * CELLS, :]
                bdq, bdg = diag_pair(fq[side, a, :, slot], fg[side, a, :, slot])
                theirs = tuple(st_in[side, a, slot, r : r + 1] for r in range(3))
                start = st_in[side, a, slot, 3:4, 0:128].astype(jnp.int32)
                add = bias(mrep[a, first * CELLS : end * CELLS, :], first - block, start)
                e, dp, stats = partial_stats(keys, values, bdq, bdg, add)
                alpha, _, delta = merged(stats, theirs)
                p, ds = weights(e, dp, alpha, delta)
                add_key_grads(a, first, end, p, ds, bdq, bdg, False)
            return carry

        lax.fori_loop(0, NA, body, 0)

    lax.fori_loop(0, NA, edge_stats, 0)
    st_copy(1).start()

    @pl.when(jnp.logical_not(first_tile))
    def _():
        st_copy(0).start()

    lax.fori_loop(0, NA, middle, 0)

    @pl.when(first_tile)
    def _():
        pl.semaphore_wait(late, 1)
        for copy in bulk(0) + [st_copy(0)]:
            copy.start()

    foreign_keys(1)
    foreign_keys(0)

    out_q = pltpu.make_async_copy(o_q, oq_hbm, out_sem.at[0])
    out_q.start()
    rsend[0] = rk_s[REG_DEV:, :]
    rsend[1] = rv_s[REG_DEV:, :]
    reg_copy = pltpu.make_async_remote_copy(
        rsend, rrecv, lat_ss.at[1], lat_rs.at[1], device_id={"lat": peer}, device_id_type=MESH
    )
    reg_copy.start()
    foreign_queries(1)
    reg_copy.wait_recv()
    own_k = (rk_s[:REG_DEV, :] + rrecv[0]) / divisor
    own_v = (rv_s[:REG_DEV, :] + rrecv[1]) / divisor
    for a in range(NA):
        for b in range(NB):
            mine = row8 == reg_ref[a, b]
            rep = mrep[a, b * CELLS : (b + 1) * CELLS, :]
            rep2 = jnp.concatenate([rep, rep], axis=1)
            for own, total, out in ((own_k, dk_s, o_k), (own_v, dv_s, o_v)):
                row = jnp.sum(jnp.where(mine, own, 0.0), axis=0, keepdims=True)
                cells = total[a, b * CELLS : (b + 1) * CELLS, :] + rep2 * row
                if b < 2:
                    total[a, b * CELLS : (b + 1) * CELLS, :] = cells
                else:
                    out[a, :, b] = cells.reshape(WIN, WIN, 256).astype(BF16)

    foreign_queries(0)
    for a in range(NA):
        for b in range(2):
            for total, out in ((dk_s, o_k), (dv_s, o_v)):
                cells = total[a, b * CELLS : (b + 1) * CELLS, :]
                out[a, :, b] = cells.reshape(WIN, WIN, 256).astype(BF16)
    out_k = pltpu.make_async_copy(o_k, ok_hbm, out_sem.at[1])
    out_v = pltpu.make_async_copy(o_v, ov_hbm, out_sem.at[2])
    out_k.start()
    out_v.start()
    for side in range(2):
        for copy in bulk(side) + [st_copy(side)]:
            copy.wait_send()
    pool_copy.wait_send()
    reg_copy.wait_send()
    out_q.wait()
    out_k.wait()
    out_v.wait()


def store(a_in, b_in, c_in, a_out, b_out, c_out, stage, in_sem, out_sem):
    ins = (a_in, b_in, c_in)
    outs = (a_out, b_out, c_out)
    reads = [pltpu.make_async_copy(ins[i], stage.at[i], in_sem.at[i]) for i in range(3)]
    writes = [pltpu.make_async_copy(stage.at[i], outs[i], out_sem.at[i]) for i in range(3)]
    for copy in reads:
        copy.start()
    for read, write in zip(reads, writes):
        read.wait()
        write.start()
    for copy in writes:
        copy.wait()


def local(queries, keys, values, grad_out, key_mask, offsets, regions):
    shape = queries.shape
    grid = (NA, WIN, NB, WIN, 256)
    edge = (2, NA, WIN, 2, WIN, 256)
    hbm_spec = pl.BlockSpec(memory_space=pltpu.HBM)
    vm = pltpu.VMEM
    dma = pltpu.SemaphoreType.DMA
    outs = pl.pallas_call(
        kernel,
        out_shape=[jax.ShapeDtypeStruct(grid, BF16)] * 3,
        in_specs=[hbm_spec] * 7,
        out_specs=[hbm_spec] * 3,
        scratch_shapes=[vm(grid, BF16)] * 4
        + [vm((NA, NB * CELLS, 256), BF16)] * 2
        + [vm((NA, NB * CELLS, 128), F32), vm((2 * CELLS, 128), F32)]
        + [vm(edge, BF16)] * 4
        + [vm((2,) + key_mask.shape, jnp.int32)]
        + [vm((NA, 4, 4 * CELLS + 2 * REG_DEV, 256), F32)] * 2
        + [vm((NA, NB * CELLS, 256), F32)] * 2
        + [vm((2 * REG_DEV, 256), F32)] * 2
        + [vm((2, 2, REG_DEV, 256), BF16)]
        + [vm((2, REG_DEV, 256), F32)] * 2
        + [vm((2, NA, 2, 8, 256), F32)] * 2
        + [vm(grid, BF16)] * 3
        + [vm(key_mask.shape, jnp.int32)]
        + [pltpu.SMEM(offsets.shape, jnp.int32)] * 2
        + [dma((7,)), dma((3,))]
        + [dma((2, 2))] * 2
        + [dma((2, NA, 2))] * 2
        + [dma((2,))] * 6
        + [pltpu.SemaphoreType.REGULAR],
        compiler_params=pltpu.CompilerParams(
            collective_id=0, has_side_effects=True, vmem_limit_bytes=VMEM_BYTES
        ),
        cost_estimate=pl.CostEstimate(flops=2200000000, bytes_accessed=2300000, transcendentals=860000),
    )(
        *(x.reshape(grid) for x in (queries, keys, values, grad_out)), key_mask, offsets, regions
    )
    outs = pl.pallas_call(
        store,
        out_shape=[jax.ShapeDtypeStruct(grid, BF16)] * 3,
        in_specs=[hbm_spec] * 3,
        out_specs=[hbm_spec] * 3,
        scratch_shapes=[vm((3,) + grid, BF16), dma((3,)), dma((3,))],
        compiler_params=pltpu.CompilerParams(vmem_limit_bytes=VMEM_BYTES),
    )(*outs)
    return tuple(x.reshape(shape) for x in outs)


def solution(mesh):
    tile = P("lat", "lon", "head")
    cells = P("lat", "lon")
    return jax.shard_map(
        local, mesh=mesh, in_specs=(tile,) * 4 + (cells,) * 3, out_specs=(tile,) * 3, check_vma=False
    )
```

```python
import jax
import jax.numpy as jnp
from jax import lax
from jax.experimental import pallas as pl
from jax.experimental.pallas import tpu as pltpu
from jax.sharding import PartitionSpec as P

HS = 64
WIN = 8
CELLS = WIN * WIN
REG_DEV = 8
NA = 2
NB = 5
VMEM_BYTES = 64236 * 1024
MASKED = -1.0e30
FLOOR = -1.0e29
SCALE = HS ** (-0.5)
MESH = pl.DeviceIdType.MESH
NT = (((1,), (1,)), ((), ()))
TN = (((0,), (0,)), ((), ()))
F32 = jnp.float32
BF16 = jnp.bfloat16

EDGE = (
    (0, 0, 3, 0, 0, 2, -2), (1, 0, 4, 0, 1, 2, -1),
    (3, 1, 5, 1, 0, 1, 5), (4, 2, 5, 1, 0, 2, 5),
)
FOREIGN = (((0, -2, 0, 1), (1, -1, 0, 2)), ((0, 5, 3, 5), (1, 6, 4, 5)))


def dot(a, b, dims=(((1,), (0,)), ((), ()))):
    return lax.dot_general(a, b, dims, preferred_element_type=F32)


def kernel(
    q_hbm, k_hbm, v_hbm, g_hbm, mask_hbm, off_hbm, reg_hbm,
    o_q, o_k, o_v,
    q_in, k_in, v_in, g_in, kb, vb, mrep, frep,
    fk, fv, fq, fg, fmask, e_s, p_s, dk_s, dv_s, rk_s, rv_s,
    pool, rsend, rrecv, st_out, st_in,
    mask_ref, off_ref, reg_ref,
    in_sem, kv_ss, kv_rs, qg_ss, qg_rs, mk_ss, mk_rs, st_ss, st_rs, lat_ss, lat_rs, late,
):
    count = lax.axis_size("lon")
    me = lax.axis_index("lon")
    right = lax.rem(me + 1, count)
    left = lax.rem(me + count - 1, count)
    peer = 1 - lax.axis_index("lat")
    sides = ({"lon": left}, {"lon": right})
    first_tile = me == 0
    last_tile = me == count - 1

    barrier = pltpu.get_barrier_semaphore()
    for device in (sides[0], {"lat": peer}):
        pl.semaphore_signal(barrier, inc=1, device_id=device, device_id_type=MESH)

    @pl.when(jnp.logical_not(last_tile))
    def _():
        pl.semaphore_signal(barrier, inc=1, device_id=sides[1], device_id_type=MESH)

    loads = [
        pltpu.make_async_copy(src, dst, in_sem.at[i])
        for i, (src, dst) in enumerate((
            (mask_hbm, mask_ref), (off_hbm, off_ref), (reg_hbm, reg_ref),
            (k_hbm, k_in), (v_hbm, v_in), (q_hbm, q_in), (g_hbm, g_in),
        ))
    ]
    for copy in loads:
        copy.start()
    pl.semaphore_wait(barrier, jnp.where(first_tile, 2, 3))

    @pl.when(last_tile)
    def _():
        pl.semaphore_signal(late, inc=1, device_id=sides[1], device_id_type=MESH)

    def edge_blocks(side):
        return pl.ds(0 if side == 0 else 3, 2)

    def remote(src, dst, ss, rs, side):
        return pltpu.make_async_remote_copy(
            src, dst, ss, rs, device_id=sides[side], device_id_type=MESH
        )

    def mask_copy(side):
        return remote(mask_hbm, fmask.at[1 - side], mk_ss.at[side], mk_rs.at[1 - side], side)

    def kv_copy(side, kind):
        src = (k_hbm, v_hbm)[kind].at[:, :, edge_blocks(side)]
        dst = (fk, fv)[kind].at[1 - side]
        return remote(src, dst, kv_ss.at[side, kind], kv_rs.at[1 - side, kind], side)

    def qg_copy(side, a, kind):
        src = (q_hbm, g_hbm)[kind].at[a, :, edge_blocks(side)]
        dst = (fq, fg)[kind].at[1 - side, a]
        return remote(src, dst, qg_ss.at[side, a, kind], qg_rs.at[1 - side, a, kind], side)

    def st_copy(side):
        return remote(st_out.at[side], st_in.at[1 - side], st_ss.at[side], st_rs.at[1 - side], side)

    def bulk(side):
        copies = [mask_copy(side)] + [kv_copy(side, kind) for kind in range(2)]
        return copies + [qg_copy(side, a, kind) for a in range(NA) for kind in range(2)]

    for copy in bulk(1):
        copy.start()

    @pl.when(jnp.logical_not(first_tile))
    def _():
        for copy in bulk(0):
            copy.start()

    lane_head = lax.broadcasted_iota(jnp.int32, (CELLS, 4 * HS), 1) // HS
    head_mask = [(lane_head == h).astype(F32).astype(BF16) for h in range(4)]
    low_half = lax.broadcasted_iota(jnp.int32, (CELLS, 128), 1) < HS

    def block_diag(x):
        return jnp.concatenate([x * head_mask[h] for h in range(4)], axis=0)

    def diag_rows(full):
        return jnp.concatenate(
            [
                jnp.where(low_half, full[0:64, 0:128], full[64:128, 0:128]),
                jnp.where(low_half, full[128:192, 128:256], full[192:256, 128:256]),
            ],
            axis=1,
        )

    for copy in loads:
        copy.wait()

    cell_t = lax.broadcasted_iota(jnp.int32, (CELLS, NB * WIN), 0) % WIN
    lane = lax.broadcasted_iota(jnp.int32, (CELLS, NB * WIN), 1)
    row8 = lax.broadcasted_iota(jnp.int32, (REG_DEV, 256), 0)

    def mask_rows(mask8):
        mask8 = mask8.astype(F32)
        return jnp.broadcast_to(mask8[:, None, :], (WIN, WIN, NB * WIN)).reshape(CELLS, NB * WIN)

    def mask_cells(mask64, b):
        column = jnp.sum(jnp.where(lane == cell_t + b * WIN, mask64, 0.0), axis=1, keepdims=True)
        return jnp.broadcast_to(column, (CELLS, 128))

    pk = jnp.zeros((REG_DEV, 256), F32)
    pv = jnp.zeros((REG_DEV, 256), F32)
    cnt = jnp.zeros((REG_DEV, 256), F32)
    for a in range(NA):
        mask64 = mask_rows(mask_ref[a * WIN : (a + 1) * WIN, :])
        for b in range(NB):
            rep = mask_cells(mask64, b)
            mrep[a, b * CELLS : (b + 1) * CELLS, :] = rep
            rep2 = jnp.concatenate([rep, rep], axis=1)
            kx = k_in[a, :, b].reshape(CELLS, 256)
            vx = v_in[a, :, b].reshape(CELLS, 256)
            kb[a, b * CELLS : (b + 1) * CELLS, :] = kx
            vb[a, b * CELLS : (b + 1) * CELLS, :] = vx
            mine = row8 == reg_ref[a, b]
            pk = pk + jnp.where(mine, jnp.sum(kx.astype(F32) * rep2, axis=0, keepdims=True), 0.0)
            pv = pv + jnp.where(mine, jnp.sum(vx.astype(F32) * rep2, axis=0, keepdims=True), 0.0)
            cnt = cnt + jnp.where(mine, jnp.sum(rep2, axis=0, keepdims=True), 0.0)
    divisor = jnp.maximum(cnt, 1.0)
    pool[0, 0] = (pk / divisor).astype(BF16)
    pool[0, 1] = (pv / divisor).astype(BF16)
    pool_copy = pltpu.make_async_remote_copy(
        pool.at[0], pool.at[1], lat_ss.at[0], lat_rs.at[0], device_id={"lat": peer}, device_id_type=MESH
    )
    pool_copy.start()
    dk_s[...] = jnp.zeros_like(dk_s)
    dv_s[...] = jnp.zeros_like(dv_s)
    rk_s[...] = jnp.zeros_like(rk_s)
    rv_s[...] = jnp.zeros_like(rv_s)
    pool_copy.wait_recv()
    reg_k = jnp.concatenate([pool[0, 0].astype(F32), pool[1, 0].astype(F32)], axis=0).astype(BF16)
    reg_v = jnp.concatenate([pool[0, 1].astype(F32), pool[1, 1].astype(F32)], axis=0).astype(BF16)

    def bias(rep, relative, start):
        row = lax.broadcasted_iota(jnp.int32, rep.shape, 0)
        key_off = row // CELLS * WIN + row % WIN + relative * WIN
        usable = (key_off >= start - WIN) & (key_off < start + 2 * WIN) & (rep > 0.5)
        half = jnp.where(usable, 0.0, MASKED)
        return jnp.concatenate([half, half], axis=1)

    def partial_stats(keys, values, bdq, bdg, add):
        s = dot(keys, bdq, NT) + add
        dp = dot(values, bdg, NT)
        top = jnp.maximum(jnp.max(s, axis=0, keepdims=True), FLOOR)
        e = jnp.exp(s - top)
        total = jnp.sum(e, axis=0, keepdims=True)
        inner = jnp.sum(e * dp, axis=0, keepdims=True)
        return e, dp, (top, total, inner)

    def merged(x, y):
        top = jnp.maximum(x[0], y[0])
        fx = jnp.exp(x[0] - top)
        fy = jnp.exp(y[0] - top)
        inverse = 1.0 / (x[1] * fx + y[1] * fy)
        return fx * inverse, fy * inverse, (x[2] * fx + y[2] * fy) * inverse

    def weights(e, dp, alpha, delta):
        p = e * alpha
        ds = p * (dp - delta)
        return p.astype(BF16), ds.astype(BF16)

    def add_key_grads(a, first, end, p, ds, bdq, bdg, regs):
        rows = (end - first) * CELLS
        dv = dot(p, bdg)
        dk = dot(ds, bdq)
        dv_s[a, first * CELLS : end * CELLS, :] += dv[:rows]
        dk_s[a, first * CELLS : end * CELLS, :] += dk[:rows]
        if regs:
            rv_s[...] += dv[rows:]
            rk_s[...] += dk[rows:]

    def diag_pair(q, g):
        bdq = block_diag(q.reshape(CELLS, 256) * jnp.asarray(SCALE, BF16))
        return bdq, block_diag(g.reshape(CELLS, 256))

    def local_q(a, block):
        return diag_pair(q_in[a, :, block], g_in[a, :, block])

    def local_keys(a, first, end):
        keys = jnp.concatenate([kb[a, first * CELLS : end * CELLS, :], reg_k], axis=0)
        values = jnp.concatenate([vb[a, first * CELLS : end * CELLS, :], reg_v], axis=0)
        return keys, values

    def local_stats(a, block, first, end):
        keys, values = local_keys(a, first, end)
        bdq, bdg = local_q(a, block)
        rep = mrep[a, first * CELLS : end * CELLS, :]
        add = jnp.concatenate(
            [bias(rep, first - block, off_ref[a, block]), jnp.zeros((2 * REG_DEV, 256), F32)], axis=0
        )
        e, dp, stats = partial_stats(keys, values, bdq, bdg, add)
        return keys, bdq, bdg, e, dp, stats

    def edge_stats(a, carry):
        for i, (block, first, end, side, _, _, _) in enumerate(EDGE):
            rows = (end - first) * CELLS + 2 * REG_DEV
            _, _, _, e, dp, stats = local_stats(a, block, first, end)
            e_s[a, i, :rows] = e
            p_s[a, i, :rows] = dp
            slot = i % 2
            for r in range(3):
                st_out[side, a, slot, r : r + 1] = stats[r]
            st_out[side, a, slot, 3:4] = jnp.full((1, 256), off_ref[a, block], jnp.int32).astype(F32)
        return carry

    def middle(a, carry):
        keys, bdq, bdg, e, dp, stats = local_stats(a, 2, 0, NB)
        inverse = 1.0 / stats[1]
        p, ds = weights(e, dp, inverse, stats[2] * inverse)
        add_key_grads(a, 0, NB, p, ds, bdq, bdg, True)
        dq = diag_rows(dot(ds, keys, TN)) * SCALE
        o_q[a, :, 2] = dq.reshape(WIN, WIN, 256).astype(BF16)
        return carry

    def foreign_keys(side):
        mask_copy(1 - side).wait_recv()
        for kind in range(2):
            kv_copy(1 - side, kind).wait_recv()

        def body(a, carry):
            mask64 = mask_rows(fmask[side, pl.ds(pl.multiple_of(a * WIN, WIN), WIN), :])
            for slot in range(2):
                frep[slot * CELLS : (slot + 1) * CELLS, :] = mask_cells(mask64, slot + (3 if side == 0 else 0))
            for i, (block, first, end, edge_side, low, high, relative) in enumerate(EDGE):
                if edge_side != side:
                    continue
                rows = (end - first) * CELLS + 2 * REG_DEV
                far_k = jnp.concatenate(
                    [fk[side, a, :, slot].reshape(CELLS, 256) for slot in range(low, high)], axis=0
                )
                far_v = jnp.concatenate(
                    [fv[side, a, :, slot].reshape(CELLS, 256) for slot in range(low, high)], axis=0
                )
                keys, _ = local_keys(a, first, end)
                bdq, bdg = local_q(a, block)
                add = bias(frep[low * CELLS : high * CELLS, :], relative - block, off_ref[a, block])
                far_e, far_dp, far = partial_stats(far_k, far_v, bdq, bdg, add)
                near = tuple(st_out[side, a, i % 2, r : r + 1] for r in range(3))
                alpha, far_alpha, delta = merged(near, far)
                p, ds = weights(e_s[a, i, :rows], p_s[a, i, :rows], alpha, delta)
                _, far_ds = weights(far_e, far_dp, far_alpha, delta)
                dq = diag_rows(dot(ds, keys, TN) + dot(far_ds, far_k, TN)) * SCALE
                add_key_grads(a, first, end, p, ds, bdq, bdg, True)
                o_q[a, :, block] = dq.reshape(WIN, WIN, 256).astype(BF16)
            return carry

        lax.fori_loop(0, NA, body, 0)

    def foreign_queries(side):
        st_copy(1 - side).wait_recv()

        def body(a, carry):
            for kind in range(2):
                qg_copy(1 - side, a, kind).wait_recv()
            for slot, block, first, end in FOREIGN[side]:
                keys = kb[a, first * CELLS : end * CELLS, :]
                values = vb[a, first * CELLS : end * CELLS, :]
                bdq, bdg = diag_pair(fq[side, a, :, slot], fg[side, a, :, slot])
                theirs = tuple(st_in[side, a, slot, r : r + 1] for r in range(3))
                start = st_in[side, a, slot, 3:4, 0:128].astype(jnp.int32)
                add = bias(mrep[a, first * CELLS : end * CELLS, :], first - block, start)
                e, dp, stats = partial_stats(keys, values, bdq, bdg, add)
                alpha, _, delta = merged(stats, theirs)
                p, ds = weights(e, dp, alpha, delta)
                add_key_grads(a, first, end, p, ds, bdq, bdg, False)
            return carry

        lax.fori_loop(0, NA, body, 0)

    lax.fori_loop(0, NA, edge_stats, 0)
    st_copy(1).start()

    @pl.when(jnp.logical_not(first_tile))
    def _():
        st_copy(0).start()

    lax.fori_loop(0, NA, middle, 0)

    @pl.when(first_tile)
    def _():
        pl.semaphore_wait(late, 1)
        for copy in bulk(0) + [st_copy(0)]:
            copy.start()

    foreign_keys(1)
    foreign_keys(0)

    rsend[0] = rk_s[REG_DEV:, :]
    rsend[1] = rv_s[REG_DEV:, :]
    reg_copy = pltpu.make_async_remote_copy(
        rsend, rrecv, lat_ss.at[1], lat_rs.at[1], device_id={"lat": peer}, device_id_type=MESH
    )
    reg_copy.start()
    foreign_queries(1)
    reg_copy.wait_recv()
    own_k = (rk_s[:REG_DEV, :] + rrecv[0]) / divisor
    own_v = (rv_s[:REG_DEV, :] + rrecv[1]) / divisor
    for a in range(NA):
        for b in range(NB):
            mine = row8 == reg_ref[a, b]
            rep = mrep[a, b * CELLS : (b + 1) * CELLS, :]
            rep2 = jnp.concatenate([rep, rep], axis=1)
            for own, total, out in ((own_k, dk_s, o_k), (own_v, dv_s, o_v)):
                row = jnp.sum(jnp.where(mine, own, 0.0), axis=0, keepdims=True)
                cells = total[a, b * CELLS : (b + 1) * CELLS, :] + rep2 * row
                if b < 2:
                    total[a, b * CELLS : (b + 1) * CELLS, :] = cells
                else:
                    out[a, :, b] = cells.reshape(WIN, WIN, 256).astype(BF16)

    foreign_queries(0)
    for a in range(NA):
        for b in range(2):
            for total, out in ((dk_s, o_k), (dv_s, o_v)):
                cells = total[a, b * CELLS : (b + 1) * CELLS, :]
                out[a, :, b] = cells.reshape(WIN, WIN, 256).astype(BF16)
    for side in range(2):
        for copy in bulk(side) + [st_copy(side)]:
            copy.wait_send()
    pool_copy.wait_send()
    reg_copy.wait_send()


def store(a_in, b_in, c_in, a_out, b_out, c_out, sem):
    pairs = ((a_in, a_out), (b_in, b_out), (c_in, c_out))
    copies = [pltpu.make_async_copy(src, dst, sem.at[i]) for i, (src, dst) in enumerate(pairs)]
    for copy in copies:
        copy.start()
    for copy in copies:
        copy.wait()


def local(queries, keys, values, grad_out, key_mask, offsets, regions):
    shape = queries.shape
    grid = (NA, WIN, NB, WIN, 256)
    edge = (2, NA, WIN, 2, WIN, 256)
    hbm_spec = pl.BlockSpec(memory_space=pltpu.HBM)
    vm = pltpu.VMEM
    dma = pltpu.SemaphoreType.DMA
    outs = pl.pallas_call(
        kernel,
        out_shape=[pltpu.VMEM(grid, BF16)] * 3,
        in_specs=[hbm_spec] * 7,
        out_specs=[pl.BlockSpec(memory_space=pltpu.VMEM)] * 3,
        scratch_shapes=[vm(grid, BF16)] * 4
        + [vm((NA, NB * CELLS, 256), BF16)] * 2
        + [vm((NA, NB * CELLS, 128), F32), vm((2 * CELLS, 128), F32)]
        + [vm(edge, BF16)] * 4
        + [vm((2,) + key_mask.shape, jnp.int32)]
        + [vm((NA, 4, 4 * CELLS + 2 * REG_DEV, 256), F32)] * 2
        + [vm((NA, NB * CELLS, 256), F32)] * 2
        + [vm((2 * REG_DEV, 256), F32)] * 2
        + [vm((2, 2, REG_DEV, 256), BF16)]
        + [vm((2, REG_DEV, 256), F32)] * 2
        + [vm((2, NA, 2, 8, 256), F32)] * 2
        + [vm(key_mask.shape, jnp.int32)]
        + [pltpu.SMEM(offsets.shape, jnp.int32)] * 2
        + [dma((7,))]
        + [dma((2, 2))] * 2
        + [dma((2, NA, 2))] * 2
        + [dma((2,))] * 6
        + [pltpu.SemaphoreType.REGULAR],
        compiler_params=pltpu.CompilerParams(
            collective_id=0, has_side_effects=True, vmem_limit_bytes=VMEM_BYTES
        ),
        cost_estimate=pl.CostEstimate(flops=2200000000, bytes_accessed=2300000, transcendentals=860000),
    )(
        *(x.reshape(grid) for x in (queries, keys, values, grad_out)), key_mask, offsets, regions
    )
    outs = pl.pallas_call(
        store,
        out_shape=[jax.ShapeDtypeStruct(grid, BF16)] * 3,
        in_specs=[pl.BlockSpec(memory_space=pl.ANY)] * 3,
        out_specs=[hbm_spec] * 3,
        scratch_shapes=[dma((3,))],
        compiler_params=pltpu.CompilerParams(vmem_limit_bytes=1024 * 1024),
    )(*outs)
    return tuple(x.reshape(shape) for x in outs)


def solution(mesh):
    tile = P("lat", "lon", "head")
    cells = P("lat", "lon")
    return jax.shard_map(
        local, mesh=mesh, in_specs=(tile,) * 4 + (cells,) * 3, out_specs=(tile,) * 3, check_vma=False
    )
```

```python
import jax
import jax.numpy as jnp
from jax import lax
from jax.experimental import pallas as pl
from jax.experimental.pallas import tpu as pltpu
from jax.sharding import PartitionSpec as P

HS = 64
WIN = 8
CELLS = WIN * WIN
REG_DEV = 8
NA = 2
NB = 5
VMEM_BYTES = 56 * 1024 * 1024
MASKED = -1.0e30
FLOOR = -1.0e29
SCALE = HS ** (-0.5)
MESH = pl.DeviceIdType.MESH
NT = (((1,), (1,)), ((), ()))
TN = (((0,), (0,)), ((), ()))
F32 = jnp.float32
BF16 = jnp.bfloat16

EDGE = (
    (0, 0, 3, 0, 0, 2, -2), (1, 0, 4, 0, 1, 2, -1),
    (3, 1, 5, 1, 0, 1, 5), (4, 2, 5, 1, 0, 2, 5),
)


def dot(a, b, dims=(((1,), (0,)), ((), ()))):
    return lax.dot_general(a, b, dims, preferred_element_type=F32)


def kernel(
    q_hbm, k_hbm, v_hbm, g_hbm, mask_hbm, off_hbm, reg_hbm,
    o_q, o_k, o_v,
    q_in, k_in, v_in, g_in, kb, vb, mrep, frep,
    fk, fv, fq, fg, fmask, e_s, p_s, dk_s, dv_s, rk_s, rv_s,
    pool, rsend, rrecv, st_out, st_in,
    mask_ref, off_ref, reg_ref,
    in_sem, kv_ss, kv_rs, qg_ss, qg_rs, mk_ss, mk_rs, st_ss, st_rs, lat_ss, lat_rs, late, go, chain, peer_in,
):
    count = lax.axis_size("lon")
    me = lax.axis_index("lon")
    right = lax.rem(me + 1, count)
    left = lax.rem(me + count - 1, count)
    peer = 1 - lax.axis_index("lat")
    sides = ({"lon": left}, {"lon": right})
    first_tile = me == 0
    last_tile = me == count - 1

    before_last = me == count - 2

    barrier = pltpu.get_barrier_semaphore()
    pl.semaphore_signal(barrier, inc=1, device_id=sides[0], device_id_type=MESH)

    @pl.when(me < count - 2)
    def _():
        pl.semaphore_signal(barrier, inc=1, device_id=sides[1], device_id_type=MESH)

    @pl.when(jnp.logical_not(last_tile))
    def _():
        pl.semaphore_signal(barrier, inc=1, device_id={"lat": peer}, device_id_type=MESH)

    pl.semaphore_wait(barrier, jnp.where(last_tile, 1, jnp.where(first_tile, 2, 3)))

    @pl.when(last_tile)
    def _():
        pl.semaphore_signal(late, inc=1, device_id=sides[1], device_id_type=MESH)

    @pl.when(before_last)
    def _():
        pl.semaphore_signal(chain, inc=1, device_id={"lat": peer}, device_id_type=MESH)
        pl.semaphore_signal(go, inc=1, device_id=sides[1], device_id_type=MESH)

    loads = [
        pltpu.make_async_copy(src, dst, in_sem.at[i])
        for i, (src, dst) in enumerate((
            (mask_hbm, mask_ref), (off_hbm, off_ref), (reg_hbm, reg_ref),
            (k_hbm, k_in), (v_hbm, v_in), (q_hbm, q_in), (g_hbm, g_in),
        ))
    ]

    def edge_blocks(side):
        return pl.ds(3 * side, 2)

    def remote(src, dst, ss, rs, side):
        return pltpu.make_async_remote_copy(
            src, dst, ss, rs, device_id={"lon": jnp.where(side == 0, left, right)}, device_id_type=MESH
        )

    def mask_copy(side):
        return remote(mask_hbm, fmask.at[1 - side], mk_ss.at[side], mk_rs.at[1 - side], side)

    def kv_copy(side, kind):
        src = (k_hbm, v_hbm)[kind].at[:, :, edge_blocks(side)]
        dst = (fk, fv)[kind].at[1 - side]
        return remote(src, dst, kv_ss.at[side, kind], kv_rs.at[1 - side, kind], side)

    def qg_copy(side, a, kind):
        src = (q_hbm, g_hbm)[kind].at[a, :, edge_blocks(side)]
        dst = (fq, fg)[kind].at[1 - side, a]
        return remote(src, dst, qg_ss.at[side, a, kind], qg_rs.at[1 - side, a, kind], side)

    def st_copy(side):
        return remote(st_out.at[side], st_in.at[1 - side], st_ss.at[side], st_rs.at[1 - side], side)

    def early(side):
        copies = [kv_copy(side, kind) for kind in range(2)] + [mask_copy(side)]
        return copies + [qg_copy(side, 0, kind) for kind in range(2)]

    def later(side):
        return [st_copy(side)] + [qg_copy(side, 1, kind) for kind in range(2)]

    for copy in early(1) + loads:
        copy.start()

    @pl.when(jnp.logical_not(first_tile | last_tile))
    def _():
        for copy in early(0):
            copy.start()

    @pl.when(before_last)
    def _():
        pl.semaphore_wait(chain, 1)
        pl.semaphore_signal(peer_in, inc=1, device_id=sides[1], device_id_type=MESH)

    lane_head = lax.broadcasted_iota(jnp.int32, (CELLS, 4 * HS), 1) // HS
    head_mask = [(lane_head == h).astype(F32).astype(BF16) for h in range(4)]
    low_half = lax.broadcasted_iota(jnp.int32, (CELLS, 128), 1) < HS

    def block_diag(x):
        return jnp.concatenate([x * head_mask[h] for h in range(4)], axis=0)

    def diag_rows(full):
        return jnp.concatenate(
            [
                jnp.where(low_half, full[0:64, 0:128], full[64:128, 0:128]),
                jnp.where(low_half, full[128:192, 128:256], full[192:256, 128:256]),
            ],
            axis=1,
        )

    for copy in loads:
        copy.wait()

    cell_t = lax.broadcasted_iota(jnp.int32, (CELLS, NB * WIN), 0) % WIN
    lane = lax.broadcasted_iota(jnp.int32, (CELLS, NB * WIN), 1)
    row8 = lax.broadcasted_iota(jnp.int32, (REG_DEV, 256), 0)

    def mask_rows(mask8):
        mask8 = mask8.astype(F32)
        return jnp.broadcast_to(mask8[:, None, :], (WIN, WIN, NB * WIN)).reshape(CELLS, NB * WIN)

    def mask_cells(mask64, b):
        column = jnp.sum(jnp.where(lane == cell_t + b * WIN, mask64, 0.0), axis=1, keepdims=True)
        return jnp.broadcast_to(column, (CELLS, 128))

    pk = jnp.zeros((REG_DEV, 256), F32)
    pv = jnp.zeros((REG_DEV, 256), F32)
    cnt = jnp.zeros((REG_DEV, 256), F32)
    for a in range(NA):
        mask64 = mask_rows(mask_ref[a * WIN : (a + 1) * WIN, :])
        for b in range(NB):
            rep = mask_cells(mask64, b)
            mrep[a, b * CELLS : (b + 1) * CELLS, :] = rep
            rep2 = jnp.concatenate([rep, rep], axis=1)
            kx = k_in[a, :, b].reshape(CELLS, 256)
            vx = v_in[a, :, b].reshape(CELLS, 256)
            kb[a, b * CELLS : (b + 1) * CELLS, :] = kx
            vb[a, b * CELLS : (b + 1) * CELLS, :] = vx
            mine = row8 == reg_ref[a, b]
            pk = pk + jnp.where(mine, jnp.sum(kx.astype(F32) * rep2, axis=0, keepdims=True), 0.0)
            pv = pv + jnp.where(mine, jnp.sum(vx.astype(F32) * rep2, axis=0, keepdims=True), 0.0)
            cnt = cnt + jnp.where(mine, jnp.sum(rep2, axis=0, keepdims=True), 0.0)
    divisor = jnp.maximum(cnt, 1.0)
    pool[0, 0] = (pk / divisor).astype(BF16)
    pool[0, 1] = (pv / divisor).astype(BF16)
    pool_copy = pltpu.make_async_remote_copy(
        pool.at[0], pool.at[1], lat_ss.at[0], lat_rs.at[0], device_id={"lat": peer}, device_id_type=MESH
    )

    @pl.when(last_tile)
    def _():
        pl.semaphore_wait(go, 1)
        for copy in early(0):
            copy.start()
        pl.semaphore_wait(peer_in, 1)

    pool_copy.start()
    dk_s[...] = jnp.zeros_like(dk_s)
    dv_s[...] = jnp.zeros_like(dv_s)
    rk_s[...] = jnp.zeros_like(rk_s)
    rv_s[...] = jnp.zeros_like(rv_s)
    pool_copy.wait_recv()
    reg_k = jnp.concatenate([pool[0, 0].astype(F32), pool[1, 0].astype(F32)], axis=0).astype(BF16)
    reg_v = jnp.concatenate([pool[0, 1].astype(F32), pool[1, 1].astype(F32)], axis=0).astype(BF16)

    def bias(rep, relative, start):
        row = lax.broadcasted_iota(jnp.int32, rep.shape, 0)
        key_off = row // CELLS * WIN + row % WIN + relative * WIN
        usable = (key_off >= start - WIN) & (key_off < start + 2 * WIN) & (rep > 0.5)
        half = jnp.where(usable, 0.0, MASKED)
        return jnp.concatenate([half, half], axis=1)

    def partial_stats(keys, values, bdq, bdg, add):
        s = dot(keys, bdq, NT) + add
        dp = dot(values, bdg, NT)
        top = jnp.maximum(jnp.max(s, axis=0, keepdims=True), FLOOR)
        e = jnp.exp(s - top)
        total = jnp.sum(e, axis=0, keepdims=True)
        inner = jnp.sum(e * dp, axis=0, keepdims=True)
        return e, dp, (top, total, inner)

    def merged(x, y):
        top = jnp.maximum(x[0], y[0])
        fx = jnp.exp(x[0] - top)
        fy = jnp.exp(y[0] - top)
        inverse = 1.0 / (x[1] * fx + y[1] * fy)
        return fx * inverse, fy * inverse, (x[2] * fx + y[2] * fy) * inverse

    def weights(e, dp, alpha, delta):
        p = e * alpha
        ds = p * (dp - delta)
        return p.astype(BF16), ds.astype(BF16)

    def add_key_grads(a, first, end, p, ds, bdq, bdg, regs):
        rows = (end - first) * CELLS
        dv = dot(p, bdg)
        dk = dot(ds, bdq)
        dv_s[a, first * CELLS : end * CELLS, :] += dv[:rows]
        dk_s[a, first * CELLS : end * CELLS, :] += dk[:rows]
        if regs:
            rv_s[...] += dv[rows:]
            rk_s[...] += dk[rows:]

    def diag_pair(q, g):
        bdq = block_diag(q.reshape(CELLS, 256) * jnp.asarray(SCALE, BF16))
        return bdq, block_diag(g.reshape(CELLS, 256))

    def local_q(a, block):
        return diag_pair(q_in[a, :, block], g_in[a, :, block])

    def local_keys(a, first, end):
        keys = jnp.concatenate([kb[a, first * CELLS : end * CELLS, :], reg_k], axis=0)
        values = jnp.concatenate([vb[a, first * CELLS : end * CELLS, :], reg_v], axis=0)
        return keys, values

    def local_stats(a, block, first, end):
        keys, values = local_keys(a, first, end)
        bdq, bdg = local_q(a, block)
        rep = mrep[a, first * CELLS : end * CELLS, :]
        add = jnp.concatenate(
            [bias(rep, first - block, off_ref[a, block]), jnp.zeros((2 * REG_DEV, 256), F32)], axis=0
        )
        e, dp, stats = partial_stats(keys, values, bdq, bdg, add)
        return keys, bdq, bdg, e, dp, stats

    def edge_stats(a, carry):
        for i, (block, first, end, side, _, _, _) in enumerate(EDGE):
            rows = (end - first) * CELLS + 2 * REG_DEV
            _, _, _, e, dp, stats = local_stats(a, block, first, end)
            e_s[a, i, :rows] = e
            p_s[a, i, :rows] = dp
            slot = i % 2
            for r in range(3):
                st_out[side, a, slot, r : r + 1] = stats[r]
            st_out[side, a, slot, 3:4] = jnp.full((1, 256), off_ref[a, block], jnp.int32).astype(F32)
        return carry

    def middle(a, carry):
        keys, bdq, bdg, e, dp, stats = local_stats(a, 2, 0, NB)
        inverse = 1.0 / stats[1]
        p, ds = weights(e, dp, inverse, stats[2] * inverse)
        add_key_grads(a, 0, NB, p, ds, bdq, bdg, True)
        dq = diag_rows(dot(ds, keys, TN)) * SCALE
        o_q[a, :, 2] = dq.reshape(WIN, WIN, 256).astype(BF16)
        return carry

    def foreign_keys(side):
        mask_copy(1 - side).wait_recv()
        for kind in range(2):
            kv_copy(1 - side, kind).wait_recv()

        def body(a, carry):
            mask64 = mask_rows(fmask[side, pl.ds(pl.multiple_of(a * WIN, WIN), WIN), :])
            for slot in range(2):
                frep[slot * CELLS : (slot + 1) * CELLS, :] = mask_cells(mask64, slot + (3 if side == 0 else 0))
            for i, (block, first, end, edge_side, low, high, relative) in enumerate(EDGE):
                if edge_side != side:
                    continue
                rows = (end - first) * CELLS + 2 * REG_DEV
                far_k = jnp.concatenate(
                    [fk[side, a, :, slot].reshape(CELLS, 256) for slot in range(low, high)], axis=0
                )
                far_v = jnp.concatenate(
                    [fv[side, a, :, slot].reshape(CELLS, 256) for slot in range(low, high)], axis=0
                )
                keys, _ = local_keys(a, first, end)
                bdq, bdg = local_q(a, block)
                add = bias(frep[low * CELLS : high * CELLS, :], relative - block, off_ref[a, block])
                far_e, far_dp, far = partial_stats(far_k, far_v, bdq, bdg, add)
                near = tuple(st_out[side, a, i % 2, r : r + 1] for r in range(3))
                alpha, far_alpha, delta = merged(near, far)
                p, ds = weights(e_s[a, i, :rows], p_s[a, i, :rows], alpha, delta)
                _, far_ds = weights(far_e, far_dp, far_alpha, delta)
                dq = diag_rows(dot(ds, keys, TN) + dot(far_ds, far_k, TN)) * SCALE
                add_key_grads(a, first, end, p, ds, bdq, bdg, True)
                o_q[a, :, block] = dq.reshape(WIN, WIN, 256).astype(BF16)
            return carry

        lax.fori_loop(0, NA, body, 0)

    def foreign_queries(side, a):
        for kind in range(2):
            qg_copy(1 - side, a, kind).wait_recv()
        for blocks in range(1, 3):
            slot = blocks - 1 + side * (3 - 2 * blocks)
            first = side * (NB - blocks)
            relative = jnp.where(side == 0, blocks - 3, 7 - blocks)
            cells = pl.ds(pl.multiple_of(first * CELLS, CELLS), blocks * CELLS)
            bdq, bdg = diag_pair(fq[side, a, :, slot], fg[side, a, :, slot])
            theirs = tuple(st_in[side, a, slot, r : r + 1] for r in range(3))
            start = st_in[side, a, slot, 3:4, 0:128].astype(jnp.int32)
            add = bias(mrep[a, cells, :], first - relative, start)
            e, dp, stats = partial_stats(kb[a, cells, :], vb[a, cells, :], bdq, bdg, add)
            alpha, _, delta = merged(stats, theirs)
            p, ds = weights(e, dp, alpha, delta)
            dv_s[a, cells, :] += dot(p, bdg)
            dk_s[a, cells, :] += dot(ds, bdq)

    def spread(a, low, high):
        for b in range(low, high):
            mine = row8 == reg_ref[a, b]
            rep = mrep[a, b * CELLS : (b + 1) * CELLS, :]
            rep2 = jnp.concatenate([rep, rep], axis=1)
            for own, total, out in ((rrecv[0], dk_s, o_k), (rrecv[1], dv_s, o_v)):
                row = jnp.sum(jnp.where(mine, own, 0.0), axis=0, keepdims=True)
                cells = total[a, b * CELLS : (b + 1) * CELLS, :] + rep2 * row
                out[a, :, b] = cells.reshape(WIN, WIN, 256).astype(BF16)

    lax.fori_loop(0, NA, edge_stats, 0)
    for copy in later(1):
        copy.start()

    @pl.when(jnp.logical_not(first_tile))
    def _():
        for copy in later(0):
            copy.start()

    lax.fori_loop(0, NA, middle, 0)

    @pl.when(first_tile)
    def _():
        pl.semaphore_wait(late, 1)
        for copy in early(0) + later(0):
            copy.start()

    reg_copy = pltpu.make_async_remote_copy(
        rsend, rrecv, lat_ss.at[1], lat_rs.at[1], device_id={"lat": peer}, device_id_type=MESH
    )
    foreign_keys(1)

    def step(i, carry):
        keys_now = i == jnp.where(first_tile, 2, 0)
        number = jnp.where(first_tile & (i < 2), i + 1, i) - 1
        side = jnp.where(first_tile, (i < 2).astype(jnp.int32), 1 - lax.rem(number + 4, 2))
        a = jnp.where(first_tile, jnp.where(i < 2, i, i - 3), lax.div(number + 4, 2) - 2)

        @pl.when(keys_now)
        def _():
            foreign_keys(0)
            rsend[0] = rk_s[REG_DEV:, :]
            rsend[1] = rv_s[REG_DEV:, :]
            reg_copy.start()

        @pl.when(jnp.logical_not(keys_now))
        def _():
            @pl.when(a == 0)
            def _():
                st_copy(1 - side).wait_recv()

            foreign_queries(side, a)

        @pl.when(jnp.logical_not(keys_now) & (side == 0) & (a == 0))
        def _():
            reg_copy.wait_recv()
            rrecv[0] = (rk_s[:REG_DEV, :] + rrecv[0]) / divisor
            rrecv[1] = (rv_s[:REG_DEV, :] + rrecv[1]) / divisor
            spread(0, 0, NB)
            spread(1, 2, 3)

        @pl.when(i == 3)
        def _():
            spread(1, 3, NB)

        return carry

    lax.fori_loop(0, 5, step, 0)
    spread(1, 0, 2)
    for side in range(2):
        for copy in early(side) + later(side):
            copy.wait_send()
    pool_copy.wait_send()
    reg_copy.wait_send()


def store(a_in, b_in, c_in, a_out, b_out, c_out, sem):
    pairs = ((a_in, a_out), (b_in, b_out), (c_in, c_out))
    copies = [pltpu.make_async_copy(src, dst, sem.at[i]) for i, (src, dst) in enumerate(pairs)]
    for copy in copies:
        copy.start()
    for copy in copies:
        copy.wait()


def local(queries, keys, values, grad_out, key_mask, offsets, regions):
    shape = queries.shape
    grid = (NA, WIN, NB, WIN, 256)
    edge = (2, NA, WIN, 2, WIN, 256)
    hbm_spec = pl.BlockSpec(memory_space=pltpu.HBM)
    vm = pltpu.VMEM
    dma = pltpu.SemaphoreType.DMA
    outs = pl.pallas_call(
        kernel,
        out_shape=[pltpu.VMEM(grid, BF16)] * 3,
        in_specs=[hbm_spec] * 7,
        out_specs=[pl.BlockSpec(memory_space=pltpu.VMEM)] * 3,
        scratch_shapes=[vm(grid, BF16)] * 4
        + [vm((NA, NB * CELLS, 256), BF16)] * 2
        + [vm((NA, NB * CELLS, 128), F32), vm((2 * CELLS, 128), F32)]
        + [vm(edge, BF16)] * 4
        + [vm((2,) + key_mask.shape, jnp.int32)]
        + [vm((NA, 4, 4 * CELLS + 2 * REG_DEV, 256), F32)] * 2
        + [vm((NA, NB * CELLS, 256), F32)] * 2
        + [vm((2 * REG_DEV, 256), F32)] * 2
        + [vm((2, 2, REG_DEV, 256), BF16)]
        + [vm((2, REG_DEV, 256), F32)] * 2
        + [vm((2, NA, 2, 8, 256), F32)] * 2
        + [vm(key_mask.shape, jnp.int32)]
        + [pltpu.SMEM(offsets.shape, jnp.int32)] * 2
        + [dma((7,))]
        + [dma((2, 2))] * 2
        + [dma((2, NA, 2))] * 2
        + [dma((2,))] * 6
        + [pltpu.SemaphoreType.REGULAR] * 4,
        compiler_params=pltpu.CompilerParams(
            collective_id=0, has_side_effects=True, vmem_limit_bytes=VMEM_BYTES
        ),
        cost_estimate=pl.CostEstimate(flops=2200000000, bytes_accessed=2300000, transcendentals=860000),
    )(
        *(x.reshape(grid) for x in (queries, keys, values, grad_out)), key_mask, offsets, regions
    )
    outs = pl.pallas_call(
        store,
        out_shape=[jax.ShapeDtypeStruct(grid, BF16)] * 3,
        in_specs=[pl.BlockSpec(memory_space=pl.ANY)] * 3,
        out_specs=[hbm_spec] * 3,
        scratch_shapes=[dma((3,))],
        compiler_params=pltpu.CompilerParams(vmem_limit_bytes=1024 * 1024),
    )(*outs)
    return tuple(x.reshape(shape) for x in outs)


def solution(mesh):
    tile = P("lat", "lon", "head")
    cells = P("lat", "lon")
    return jax.shard_map(
        local, mesh=mesh, in_specs=(tile,) * 4 + (cells,) * 3, out_specs=(tile,) * 3, check_vma=False
    )
```

```python
import jax
import jax.numpy as jnp
from jax import lax
from jax.experimental import pallas as pl
from jax.experimental.pallas import tpu as pltpu
from jax.sharding import PartitionSpec as P

HS = 64
WIN = 8
CELLS = WIN * WIN
REG_DEV = 8
NA = 2
NB = 5
VMEM_BYTES = 56 * 1024 * 1024
MASKED = -1.0e30
FLOOR = -1.0e29
SCALE = HS ** (-0.5)
MESH = pl.DeviceIdType.MESH
NT = (((1,), (1,)), ((), ()))
TN = (((0,), (0,)), ((), ()))
F32 = jnp.float32
BF16 = jnp.bfloat16

EDGE = (
    (0, 0, 3, 0, 0, 2, -2), (1, 0, 4, 0, 1, 2, -1),
    (3, 1, 5, 1, 0, 1, 5), (4, 2, 5, 1, 0, 2, 5),
)


def dot(a, b, dims=(((1,), (0,)), ((), ()))):
    return lax.dot_general(a, b, dims, preferred_element_type=F32)


def kernel(
    q_hbm, k_hbm, v_hbm, g_hbm, mask_hbm, off_hbm, reg_hbm,
    o_q, o_k, o_v,
    q_in, k_in, v_in, g_in, kb, vb, mrep, frep,
    fk, fv, fq, fg, fmask, e_s, p_s, dk_s, dv_s, rk_s, rv_s,
    pool, rsend, rrecv, own_st, st_out, st_in, far_off,
    mask_ref, off_ref, reg_ref,
    in_sem, kv_ss, kv_rs, qg_ss, qg_rs, mk_ss, mk_rs, st_ss, st_rs, of_ss, of_rs, one_ss, one_rs, lat_ss, lat_rs, late, go, chain, peer_in,
):
    count = lax.axis_size("lon")
    me = lax.axis_index("lon")
    right = lax.rem(me + 1, count)
    left = lax.rem(me + count - 1, count)
    peer = 1 - lax.axis_index("lat")
    sides = ({"lon": left}, {"lon": right})
    first_tile = me == 0
    last_tile = me == count - 1

    before_last = me == count - 2

    barrier = pltpu.get_barrier_semaphore()
    pl.semaphore_signal(barrier, inc=1, device_id=sides[0], device_id_type=MESH)

    @pl.when(me < count - 2)
    def _():
        pl.semaphore_signal(barrier, inc=1, device_id=sides[1], device_id_type=MESH)

    @pl.when(jnp.logical_not(last_tile))
    def _():
        pl.semaphore_signal(barrier, inc=1, device_id={"lat": peer}, device_id_type=MESH)

    pl.semaphore_wait(barrier, jnp.where(last_tile, 1, jnp.where(first_tile, 2, 3)))

    @pl.when(last_tile)
    def _():
        pl.semaphore_signal(late, inc=1, device_id=sides[1], device_id_type=MESH)

    @pl.when(before_last)
    def _():
        pl.semaphore_signal(chain, inc=1, device_id={"lat": peer}, device_id_type=MESH)
        pl.semaphore_signal(go, inc=1, device_id=sides[1], device_id_type=MESH)

    loads = [
        pltpu.make_async_copy(src, dst, in_sem.at[i])
        for i, (src, dst) in enumerate((
            (mask_hbm, mask_ref), (off_hbm, off_ref), (reg_hbm, reg_ref),
            (k_hbm, k_in), (v_hbm, v_in), (q_hbm, q_in), (g_hbm, g_in),
        ))
    ]

    def edge_blocks(side):
        return pl.ds(3 * side, 2)

    def remote(src, dst, ss, rs, side):
        return pltpu.make_async_remote_copy(
            src, dst, ss, rs, device_id={"lon": jnp.where(side == 0, left, right)}, device_id_type=MESH
        )

    def mask_copy(side):
        return remote(mask_hbm, fmask.at[1 - side], mk_ss.at[side], mk_rs.at[1 - side], side)

    def kv_copy(side, kind):
        src = (k_hbm, v_hbm)[kind].at[:, :, edge_blocks(side)]
        dst = (fk, fv)[kind].at[1 - side]
        return remote(src, dst, kv_ss.at[side, kind], kv_rs.at[1 - side, kind], side)

    def qg_copy(side, a, kind):
        src = (q_hbm, g_hbm)[kind].at[a, :, edge_blocks(side)]
        dst = (fq, fg)[kind].at[1 - side, a]
        return remote(src, dst, qg_ss.at[side, a, kind], qg_rs.at[1 - side, a, kind], side)

    def offset_copy(side):
        return remote(off_hbm, far_off.at[1 - side], of_ss.at[side], of_rs.at[1 - side], side)

    def one_copy(side, slot, kind):
        src = (q_hbm, g_hbm)[kind].at[1, :, 3 * side + slot]
        dst = (fq, fg)[kind].at[1 - side, 1, :, slot]
        return remote(src, dst, one_ss.at[side, slot, kind], one_rs.at[1 - side, slot, kind], side)

    def st_copy(side):
        return remote(st_out.at[side], st_in.at[1 - side], st_ss.at[side], st_rs.at[1 - side], side)

    def early(side):
        copies = [kv_copy(side, kind) for kind in range(2)] + [mask_copy(side), offset_copy(side)]
        return copies + [qg_copy(side, 0, kind) for kind in range(2)]

    def later(side):
        outer = side
        slots = (outer, 1 - outer)
        return [st_copy(side)] + [one_copy(side, slot, kind) for slot in slots for kind in range(2)]

    for copy in early(1) + loads:
        copy.start()

    @pl.when(jnp.logical_not(first_tile | last_tile))
    def _():
        for copy in early(0):
            copy.start()

    @pl.when(before_last)
    def _():
        pl.semaphore_wait(chain, 1)
        pl.semaphore_signal(peer_in, inc=1, device_id=sides[1], device_id_type=MESH)

    lane_head = lax.broadcasted_iota(jnp.int32, (CELLS, 4 * HS), 1) // HS
    head_mask = [(lane_head == h).astype(F32).astype(BF16) for h in range(4)]
    low_half = lax.broadcasted_iota(jnp.int32, (CELLS, 128), 1) < HS

    def block_diag(x):
        return jnp.concatenate([x * head_mask[h] for h in range(4)], axis=0)

    def diag_rows(full):
        return jnp.concatenate(
            [
                jnp.where(low_half, full[0:64, 0:128], full[64:128, 0:128]),
                jnp.where(low_half, full[128:192, 128:256], full[192:256, 128:256]),
            ],
            axis=1,
        )

    for copy in loads:
        copy.wait()

    cell_t = lax.broadcasted_iota(jnp.int32, (CELLS, NB * WIN), 0) % WIN
    lane = lax.broadcasted_iota(jnp.int32, (CELLS, NB * WIN), 1)
    off_row = lax.broadcasted_iota(jnp.int32, (NA, NB), 0)
    off_col = lax.broadcasted_iota(jnp.int32, (NA, NB), 1)
    row8 = lax.broadcasted_iota(jnp.int32, (REG_DEV, 256), 0)

    def mask_rows(mask8):
        mask8 = mask8.astype(F32)
        return jnp.broadcast_to(mask8[:, None, :], (WIN, WIN, NB * WIN)).reshape(CELLS, NB * WIN)

    def mask_cells(mask64, b):
        column = jnp.sum(jnp.where(lane == cell_t + b * WIN, mask64, 0.0), axis=1, keepdims=True)
        return jnp.broadcast_to(column, (CELLS, 128))

    pk = jnp.zeros((REG_DEV, 256), F32)
    pv = jnp.zeros((REG_DEV, 256), F32)
    cnt = jnp.zeros((REG_DEV, 256), F32)
    for a in range(NA):
        mask64 = mask_rows(mask_ref[a * WIN : (a + 1) * WIN, :])
        for b in range(NB):
            rep = mask_cells(mask64, b)
            mrep[a, b * CELLS : (b + 1) * CELLS, :] = rep
            rep2 = jnp.concatenate([rep, rep], axis=1)
            kx = k_in[a, :, b].reshape(CELLS, 256)
            vx = v_in[a, :, b].reshape(CELLS, 256)
            kb[a, b * CELLS : (b + 1) * CELLS, :] = kx
            vb[a, b * CELLS : (b + 1) * CELLS, :] = vx
            mine = row8 == reg_ref[a, b]
            pk = pk + jnp.where(mine, jnp.sum(kx.astype(F32) * rep2, axis=0, keepdims=True), 0.0)
            pv = pv + jnp.where(mine, jnp.sum(vx.astype(F32) * rep2, axis=0, keepdims=True), 0.0)
            cnt = cnt + jnp.where(mine, jnp.sum(rep2, axis=0, keepdims=True), 0.0)
    divisor = jnp.maximum(cnt, 1.0)
    pool[0, 0] = (pk / divisor).astype(BF16)
    pool[0, 1] = (pv / divisor).astype(BF16)
    pool_copy = pltpu.make_async_remote_copy(
        pool.at[0], pool.at[1], lat_ss.at[0], lat_rs.at[0], device_id={"lat": peer}, device_id_type=MESH
    )

    @pl.when(last_tile)
    def _():
        pl.semaphore_wait(go, 1)
        for copy in early(0):
            copy.start()
        pl.semaphore_wait(peer_in, 1)

    pool_copy.start()
    dk_s[...] = jnp.zeros_like(dk_s)
    dv_s[...] = jnp.zeros_like(dv_s)
    rk_s[...] = jnp.zeros_like(rk_s)
    rv_s[...] = jnp.zeros_like(rv_s)
    pool_copy.wait_recv()
    reg_k = jnp.concatenate([pool[0, 0].astype(F32), pool[1, 0].astype(F32)], axis=0).astype(BF16)
    reg_v = jnp.concatenate([pool[0, 1].astype(F32), pool[1, 1].astype(F32)], axis=0).astype(BF16)

    def bias(rep, relative, start):
        row = lax.broadcasted_iota(jnp.int32, rep.shape, 0)
        key_off = row // CELLS * WIN + row % WIN + relative * WIN
        usable = (key_off >= start - WIN) & (key_off < start + 2 * WIN) & (rep > 0.5)
        half = jnp.where(usable, 0.0, MASKED)
        return jnp.concatenate([half, half], axis=1)

    def partial_stats(keys, values, bdq, bdg, add):
        s = dot(keys, bdq, NT) + add
        dp = dot(values, bdg, NT)
        top = jnp.maximum(jnp.max(s, axis=0, keepdims=True), FLOOR)
        e = jnp.exp(s - top)
        total = jnp.sum(e, axis=0, keepdims=True)
        inner = jnp.sum(e * dp, axis=0, keepdims=True)
        return e, dp, (top, total, inner)

    def merged(x, y):
        top = jnp.maximum(x[0], y[0])
        fx = jnp.exp(x[0] - top)
        fy = jnp.exp(y[0] - top)
        inverse = 1.0 / (x[1] * fx + y[1] * fy)
        return fx * inverse, fy * inverse, (x[2] * fx + y[2] * fy) * inverse

    def weights(e, dp, alpha, delta):
        p = e * alpha
        ds = p * (dp - delta)
        return p.astype(BF16), ds.astype(BF16)

    def add_key_grads(a, first, end, p, ds, bdq, bdg, regs):
        rows = (end - first) * CELLS
        dv = dot(p, bdg)
        dk = dot(ds, bdq)
        dv_s[a, first * CELLS : end * CELLS, :] += dv[:rows]
        dk_s[a, first * CELLS : end * CELLS, :] += dk[:rows]
        if regs:
            rv_s[...] += dv[rows:]
            rk_s[...] += dk[rows:]

    def diag_pair(q, g):
        bdq = block_diag(q.reshape(CELLS, 256) * jnp.asarray(SCALE, BF16))
        return bdq, block_diag(g.reshape(CELLS, 256))

    def local_q(a, block):
        return diag_pair(q_in[a, :, block], g_in[a, :, block])

    def local_keys(a, first, end):
        keys = jnp.concatenate([kb[a, first * CELLS : end * CELLS, :], reg_k], axis=0)
        values = jnp.concatenate([vb[a, first * CELLS : end * CELLS, :], reg_v], axis=0)
        return keys, values

    def local_stats(a, block, first, end):
        keys, values = local_keys(a, first, end)
        bdq, bdg = local_q(a, block)
        rep = mrep[a, first * CELLS : end * CELLS, :]
        add = jnp.concatenate(
            [bias(rep, first - block, off_ref[a, block]), jnp.zeros((2 * REG_DEV, 256), F32)], axis=0
        )
        e, dp, stats = partial_stats(keys, values, bdq, bdg, add)
        return keys, bdq, bdg, e, dp, stats

    def edge_stats(a, carry):
        for i, (block, first, end, side, _, _, _) in enumerate(EDGE):
            rows = (end - first) * CELLS + 2 * REG_DEV
            _, _, _, e, dp, stats = local_stats(a, block, first, end)
            e_s[a, i, :rows] = e
            p_s[a, i, :rows] = dp
            slot = i % 2
            for r in range(3):
                own_st[side, a, slot, r : r + 1] = stats[r]
            st_out[side, a, slot, 0:1] = stats[0] + jnp.log(stats[1])
            st_out[side, a, slot, 1:2] = stats[2] / stats[1]
        return carry

    def middle(a, carry):
        keys, bdq, bdg, e, dp, stats = local_stats(a, 2, 0, NB)
        inverse = 1.0 / stats[1]
        p, ds = weights(e, dp, inverse, stats[2] * inverse)
        add_key_grads(a, 0, NB, p, ds, bdq, bdg, True)
        dq = diag_rows(dot(ds, keys, TN)) * SCALE
        o_q[a, :, 2] = dq.reshape(WIN, WIN, 256).astype(BF16)
        return carry

    def foreign_keys(side):
        mask_copy(1 - side).wait_recv()
        for kind in range(2):
            kv_copy(1 - side, kind).wait_recv()

        def body(a, carry):
            mask64 = mask_rows(fmask[side, pl.ds(pl.multiple_of(a * WIN, WIN), WIN), :])
            for slot in range(2):
                frep[slot * CELLS : (slot + 1) * CELLS, :] = mask_cells(mask64, slot + (3 if side == 0 else 0))
            for i, (block, first, end, edge_side, low, high, relative) in enumerate(EDGE):
                if edge_side != side:
                    continue
                rows = (end - first) * CELLS + 2 * REG_DEV
                far_k = jnp.concatenate(
                    [fk[side, a, :, slot].reshape(CELLS, 256) for slot in range(low, high)], axis=0
                )
                far_v = jnp.concatenate(
                    [fv[side, a, :, slot].reshape(CELLS, 256) for slot in range(low, high)], axis=0
                )
                keys, _ = local_keys(a, first, end)
                bdq, bdg = local_q(a, block)
                add = bias(frep[low * CELLS : high * CELLS, :], relative - block, off_ref[a, block])
                far_e, far_dp, far = partial_stats(far_k, far_v, bdq, bdg, add)
                near = tuple(own_st[side, a, i % 2, r : r + 1] for r in range(3))
                alpha, far_alpha, delta = merged(near, far)
                p, ds = weights(e_s[a, i, :rows], p_s[a, i, :rows], alpha, delta)
                _, far_ds = weights(far_e, far_dp, far_alpha, delta)
                dq = diag_rows(dot(ds, keys, TN) + dot(far_ds, far_k, TN)) * SCALE
                add_key_grads(a, first, end, p, ds, bdq, bdg, True)
                o_q[a, :, block] = dq.reshape(WIN, WIN, 256).astype(BF16)
            return carry

        lax.fori_loop(0, NA, body, 0)

    def far_slot(side, blocks):
        return blocks - 1 + side * (3 - 2 * blocks)

    def row0_arrived(side):
        offset_copy(1 - side).wait_recv()
        st_copy(1 - side).wait_recv()
        for kind in range(2):
            qg_copy(1 - side, 0, kind).wait_recv()

    def row1_arrived(side, blocks):
        for kind in range(2):
            one_copy(1 - side, far_slot(side, blocks), kind).wait_recv()

    def far_weights(side, a, blocks):
        slot = far_slot(side, blocks)
        first = side * (NB - blocks)
        relative = jnp.where(side == 0, blocks - 3, 7 - blocks)
        cells = rows_of(first, blocks)
        bdq, bdg = diag_pair(fq[side, a, :, slot], fg[side, a, :, slot])
        top = st_in[side, a, slot, 0:1]
        theirs = (top, jnp.ones_like(top), st_in[side, a, slot, 1:2])
        here = (off_row == a) & (off_col == slot + 3 * (1 - side))
        start = jnp.sum(
            jnp.sum(jnp.where(here, far_off[side].astype(F32), 0.0), axis=1, keepdims=True),
            axis=0, keepdims=True,
        ).astype(jnp.int32)
        add = bias(mrep[a, cells, :], first - relative, start)
        e, dp, stats = partial_stats(kb[a, cells, :], vb[a, cells, :], bdq, bdg, add)
        alpha, _, delta = merged(stats, theirs)
        return cells, bdq, bdg, weights(e, dp, alpha, delta)

    def add_far(a, unit):
        cells, bdq, bdg, (p, ds) = unit
        dv_s[a, cells, :] += dot(p, bdg)
        dk_s[a, cells, :] += dot(ds, bdq)

    def one_side(side, a):
        @pl.when(a == 0)
        def _():
            row0_arrived(side)

        for blocks in (2, 1):
            @pl.when(a == 1)
            def _():
                row1_arrived(side, blocks)

            add_far(a, far_weights(side, a, blocks))

    def both_sides(a):
        @pl.when(a == 0)
        def _():
            for side in range(2):
                row0_arrived(side)

        @pl.when(a == 1)
        def _():
            for side in range(2):
                for blocks in (2, 1):
                    row1_arrived(side, blocks)

        units = [far_weights(side, a, blocks) for blocks in (2, 1) for side in range(2)]
        for unit in units:
            add_far(a, unit)

    def rows_of(first, blocks):
        start = first * CELLS
        if not isinstance(start, int):
            start = pl.multiple_of(start, CELLS)
        return pl.ds(start, blocks * CELLS)

    def spread(a, low, high):
        for b in range(low, high):
            mine = row8 == reg_ref[a, b]
            rep = mrep[a, b * CELLS : (b + 1) * CELLS, :]
            rep2 = jnp.concatenate([rep, rep], axis=1)
            for own, total, out in ((rrecv[0], dk_s, o_k), (rrecv[1], dv_s, o_v)):
                row = jnp.sum(jnp.where(mine, own, 0.0), axis=0, keepdims=True)
                cells = total[a, b * CELLS : (b + 1) * CELLS, :] + rep2 * row
                out[a, :, b] = cells.reshape(WIN, WIN, 256).astype(BF16)

    lax.fori_loop(0, NA, edge_stats, 0)
    for copy in later(1):
        copy.start()

    @pl.when(jnp.logical_not(first_tile))
    def _():
        for copy in later(0):
            copy.start()

    lax.fori_loop(0, NA, middle, 0)

    @pl.when(first_tile)
    def _():
        pl.semaphore_wait(late, 1)
        for copy in early(0) + later(0):
            copy.start()

    reg_copy = pltpu.make_async_remote_copy(
        rsend, rrecv, lat_ss.at[1], lat_rs.at[1], device_id={"lat": peer}, device_id_type=MESH
    )
    foreign_keys(1)

    def left_keys():
        foreign_keys(0)
        rsend[0] = rk_s[REG_DEV:, :]
        rsend[1] = rv_s[REG_DEV:, :]
        reg_copy.start()

    def registers_done():
        reg_copy.wait_recv()
        rrecv[0] = (rk_s[:REG_DEV, :] + rrecv[0]) / divisor
        rrecv[1] = (rv_s[:REG_DEV, :] + rrecv[1]) / divisor

    def step(i, carry):
        @pl.when(i == jnp.where(first_tile, 2, 0))
        def _():
            left_keys()

        @pl.when(first_tile & (i != 2))
        def _():
            one_side((i < 2).astype(jnp.int32), jnp.where(i < 2, i, i - 3))

        @pl.when(jnp.logical_not(first_tile) & (i > 0))
        def _():
            both_sides(i - 1)

        @pl.when(i == jnp.where(first_tile, 3, 1))
        def _():
            registers_done()
            spread(0, 0, NB)
            spread(1, 2, 3)

        @pl.when(i == jnp.where(first_tile, 3, 2))
        def _():
            spread(1, 3, NB)

        return carry

    lax.fori_loop(0, jnp.where(first_tile, 5, 3), step, 0)
    spread(1, 0, 2)
    for side in range(2):
        for copy in early(side) + later(side):
            copy.wait_send()
    pool_copy.wait_send()
    reg_copy.wait_send()


def store(a_in, b_in, c_in, a_out, b_out, c_out, sem):
    pairs = ((a_in, a_out), (b_in, b_out), (c_in, c_out))
    copies = [pltpu.make_async_copy(src, dst, sem.at[i]) for i, (src, dst) in enumerate(pairs)]
    for copy in copies:
        copy.start()
    for copy in copies:
        copy.wait()


def local(queries, keys, values, grad_out, key_mask, offsets, regions):
    shape = queries.shape
    grid = (NA, WIN, NB, WIN, 256)
    edge = (2, NA, WIN, 2, WIN, 256)
    hbm_spec = pl.BlockSpec(memory_space=pltpu.HBM)
    vm = pltpu.VMEM
    dma = pltpu.SemaphoreType.DMA
    outs = pl.pallas_call(
        kernel,
        out_shape=[pltpu.VMEM(grid, BF16)] * 3,
        in_specs=[hbm_spec] * 7,
        out_specs=[pl.BlockSpec(memory_space=pltpu.VMEM)] * 3,
        scratch_shapes=[vm(grid, BF16)] * 4
        + [vm((NA, NB * CELLS, 256), BF16)] * 2
        + [vm((NA, NB * CELLS, 128), F32), vm((2 * CELLS, 128), F32)]
        + [vm(edge, BF16)] * 4
        + [vm((2,) + key_mask.shape, jnp.int32)]
        + [vm((NA, 4, 4 * CELLS + 2 * REG_DEV, 256), F32)] * 2
        + [vm((NA, NB * CELLS, 256), F32)] * 2
        + [vm((2 * REG_DEV, 256), F32)] * 2
        + [vm((2, 2, REG_DEV, 256), BF16)]
        + [vm((2, REG_DEV, 256), F32)] * 2
        + [vm((2, NA, 2, 8, 256), F32)]
        + [vm((2, NA, 2, 2, 256), F32)] * 2
        + [vm((2,) + offsets.shape, jnp.int32)]
        + [vm(key_mask.shape, jnp.int32)]
        + [pltpu.SMEM(offsets.shape, jnp.int32)] * 2
        + [dma((7,))]
        + [dma((2, 2))] * 2
        + [dma((2, NA, 2))] * 2
        + [dma((2,))] * 6
        + [dma((2, 2, 2))] * 2
        + [dma((2,))] * 2
        + [pltpu.SemaphoreType.REGULAR] * 4,
        compiler_params=pltpu.CompilerParams(
            collective_id=0, has_side_effects=True, vmem_limit_bytes=VMEM_BYTES
        ),
        cost_estimate=pl.CostEstimate(flops=2200000000, bytes_accessed=2300000, transcendentals=860000),
    )(
        *(x.reshape(grid) for x in (queries, keys, values, grad_out)), key_mask, offsets, regions
    )
    outs = pl.pallas_call(
        store,
        out_shape=[jax.ShapeDtypeStruct(grid, BF16)] * 3,
        in_specs=[pl.BlockSpec(memory_space=pl.ANY)] * 3,
        out_specs=[hbm_spec] * 3,
        scratch_shapes=[dma((3,))],
        compiler_params=pltpu.CompilerParams(vmem_limit_bytes=1024 * 1024),
    )(*outs)
    return tuple(x.reshape(shape) for x in outs)


def solution(mesh):
    tile = P("lat", "lon", "head")
    cells = P("lat", "lon")
    return jax.shard_map(
        local, mesh=mesh, in_specs=(tile,) * 4 + (cells,) * 3, out_specs=(tile,) * 3, check_vma=False
    )
```

```python
import jax
import jax.numpy as jnp
from jax import lax
from jax.experimental import pallas as pl
from jax.experimental.pallas import tpu as pltpu
from jax.sharding import PartitionSpec as P

HS = 64
WIN = 8
CELLS = WIN * WIN
REG_DEV = 8
NA = 2
NB = 5
VMEM_BYTES = 56 * 1024 * 1024
MASKED = -1.0e30
FLOOR = -1.0e29
SCALE = HS ** (-0.5)
MESH = pl.DeviceIdType.MESH
NT = (((1,), (1,)), ((), ()))
TN = (((0,), (0,)), ((), ()))
F32 = jnp.float32
BF16 = jnp.bfloat16

EDGE = (
    (0, 0, 3, 0, 0, 2, -2), (1, 0, 4, 0, 1, 2, -1),
    (3, 1, 5, 1, 0, 1, 5), (4, 2, 5, 1, 0, 2, 5),
)


def dot(a, b, dims=(((1,), (0,)), ((), ()))):
    return lax.dot_general(a, b, dims, preferred_element_type=F32)


def kernel(
    q_hbm, k_hbm, v_hbm, g_hbm, mask_hbm, off_hbm, reg_hbm,
    o_q, o_k, o_v,
    q_in, k_in, v_in, g_in, kb, vb, mrep, frep,
    fk, fv, fq, fg, fmask, e_s, p_s, dk_s, dv_s, rk_s, rv_s,
    pool, rsend, rrecv, own_st, st_out, st_in, far_off,
    mask_ref, off_ref, reg_ref,
    in_sem, kv_ss, kv_rs, qg_ss, qg_rs, mk_ss, mk_rs, st_ss, st_rs, of_ss, of_rs, one_ss, one_rs, lat_ss, lat_rs, late, go, chain, peer_in,
):
    count = lax.axis_size("lon")
    me = lax.axis_index("lon")
    right = lax.rem(me + 1, count)
    left = lax.rem(me + count - 1, count)
    peer = 1 - lax.axis_index("lat")
    sides = ({"lon": left}, {"lon": right})
    first_tile = me == 0
    last_tile = me == count - 1

    before_last = me == count - 2

    barrier = pltpu.get_barrier_semaphore()
    pl.semaphore_signal(barrier, inc=1, device_id=sides[0], device_id_type=MESH)

    @pl.when(me < count - 2)
    def _():
        pl.semaphore_signal(barrier, inc=1, device_id=sides[1], device_id_type=MESH)

    @pl.when(jnp.logical_not(last_tile))
    def _():
        pl.semaphore_signal(barrier, inc=1, device_id={"lat": peer}, device_id_type=MESH)

    pl.semaphore_wait(barrier, jnp.where(last_tile, 1, jnp.where(first_tile, 2, 3)))

    @pl.when(last_tile)
    def _():
        pl.semaphore_signal(late, inc=1, device_id=sides[1], device_id_type=MESH)

    @pl.when(before_last)
    def _():
        pl.semaphore_signal(chain, inc=1, device_id={"lat": peer}, device_id_type=MESH)
        pl.semaphore_signal(go, inc=1, device_id=sides[1], device_id_type=MESH)

    loads = [
        pltpu.make_async_copy(src, dst, in_sem.at[i])
        for i, (src, dst) in enumerate((
            (mask_hbm, mask_ref), (off_hbm, off_ref), (reg_hbm, reg_ref),
            (k_hbm, k_in), (v_hbm, v_in), (q_hbm, q_in), (g_hbm, g_in),
        ))
    ]

    def edge_blocks(side):
        return pl.ds(3 * side, 2)

    def remote(src, dst, ss, rs, side):
        return pltpu.make_async_remote_copy(
            src, dst, ss, rs, device_id={"lon": jnp.where(side == 0, left, right)}, device_id_type=MESH
        )

    def mask_copy(side):
        return remote(mask_hbm, fmask.at[1 - side], mk_ss.at[side], mk_rs.at[1 - side], side)

    def kv_copy(side, kind):
        src = (k_hbm, v_hbm)[kind].at[:, :, edge_blocks(side)]
        dst = (fk, fv)[kind].at[1 - side]
        return remote(src, dst, kv_ss.at[side, kind], kv_rs.at[1 - side, kind], side)

    def qg_copy(side, a, kind):
        src = (q_hbm, g_hbm)[kind].at[a, :, edge_blocks(side)]
        dst = (fq, fg)[kind].at[1 - side, a]
        return remote(src, dst, qg_ss.at[side, a, kind], qg_rs.at[1 - side, a, kind], side)

    def offset_copy(side):
        return remote(off_hbm, far_off.at[1 - side], of_ss.at[side], of_rs.at[1 - side], side)

    def one_copy(side, slot, kind):
        src = (q_hbm, g_hbm)[kind].at[1, :, 3 * side + slot]
        dst = (fq, fg)[kind].at[1 - side, 1, :, slot]
        return remote(src, dst, one_ss.at[side, slot, kind], one_rs.at[1 - side, slot, kind], side)

    def st_copy(side):
        return remote(st_out.at[side], st_in.at[1 - side], st_ss.at[side], st_rs.at[1 - side], side)

    def early(side):
        copies = [kv_copy(side, kind) for kind in range(2)] + [mask_copy(side), offset_copy(side)]
        return copies + [qg_copy(side, 0, kind) for kind in range(2)]

    def later(side):
        outer = side
        slots = (outer, 1 - outer)
        return [st_copy(side)] + [one_copy(side, slot, kind) for slot in slots for kind in range(2)]

    for copy in early(1) + loads:
        copy.start()

    @pl.when(jnp.logical_not(first_tile | last_tile))
    def _():
        for copy in early(0):
            copy.start()

    @pl.when(before_last)
    def _():
        pl.semaphore_wait(chain, 1)
        pl.semaphore_signal(peer_in, inc=1, device_id=sides[1], device_id_type=MESH)

    lane_head = lax.broadcasted_iota(jnp.int32, (CELLS, 4 * HS), 1) // HS
    head_mask = [(lane_head == h).astype(F32).astype(BF16) for h in range(4)]
    low_half = lax.broadcasted_iota(jnp.int32, (CELLS, 128), 1) < HS

    def block_diag(x):
        return jnp.concatenate([x * head_mask[h] for h in range(4)], axis=0)

    def diag_rows(full):
        return jnp.concatenate(
            [
                jnp.where(low_half, full[0:64, 0:128], full[64:128, 0:128]),
                jnp.where(low_half, full[128:192, 128:256], full[192:256, 128:256]),
            ],
            axis=1,
        )

    for copy in loads:
        copy.wait()

    cell_t = lax.broadcasted_iota(jnp.int32, (CELLS, NB * WIN), 0) % WIN
    lane = lax.broadcasted_iota(jnp.int32, (CELLS, NB * WIN), 1)
    off_row = lax.broadcasted_iota(jnp.int32, (NA, NB), 0)
    off_col = lax.broadcasted_iota(jnp.int32, (NA, NB), 1)
    row8 = lax.broadcasted_iota(jnp.int32, (REG_DEV, 256), 0)

    def mask_rows(mask8):
        mask8 = mask8.astype(F32)
        return jnp.broadcast_to(mask8[:, None, :], (WIN, WIN, NB * WIN)).reshape(CELLS, NB * WIN)

    def mask_cells(mask64, b):
        column = jnp.sum(jnp.where(lane == cell_t + b * WIN, mask64, 0.0), axis=1, keepdims=True)
        return jnp.broadcast_to(column, (CELLS, 128))

    pk = jnp.zeros((REG_DEV, 256), F32)
    pv = jnp.zeros((REG_DEV, 256), F32)
    cnt = jnp.zeros((REG_DEV, 256), F32)
    for a in range(NA):
        mask64 = mask_rows(mask_ref[a * WIN : (a + 1) * WIN, :])
        for b in range(NB):
            rep = mask_cells(mask64, b)
            mrep[a, b * CELLS : (b + 1) * CELLS, :] = rep
            rep2 = jnp.concatenate([rep, rep], axis=1)
            kx = k_in[a, :, b].reshape(CELLS, 256)
            vx = v_in[a, :, b].reshape(CELLS, 256)
            kb[a, b * CELLS : (b + 1) * CELLS, :] = kx
            vb[a, b * CELLS : (b + 1) * CELLS, :] = vx
            mine = row8 == reg_ref[a, b]
            pk = pk + jnp.where(mine, jnp.sum(kx.astype(F32) * rep2, axis=0, keepdims=True), 0.0)
            pv = pv + jnp.where(mine, jnp.sum(vx.astype(F32) * rep2, axis=0, keepdims=True), 0.0)
            cnt = cnt + jnp.where(mine, jnp.sum(rep2, axis=0, keepdims=True), 0.0)
    divisor = jnp.maximum(cnt, 1.0)
    pool[0, 0] = (pk / divisor).astype(BF16)
    pool[0, 1] = (pv / divisor).astype(BF16)
    pool_copy = pltpu.make_async_remote_copy(
        pool.at[0], pool.at[1], lat_ss.at[0], lat_rs.at[0], device_id={"lat": peer}, device_id_type=MESH
    )

    @pl.when(last_tile)
    def _():
        pl.semaphore_wait(go, 1)
        for copy in early(0):
            copy.start()
        pl.semaphore_wait(peer_in, 1)

    pool_copy.start()
    dk_s[...] = jnp.zeros_like(dk_s)
    dv_s[...] = jnp.zeros_like(dv_s)
    rk_s[...] = jnp.zeros_like(rk_s)
    rv_s[...] = jnp.zeros_like(rv_s)
    pool_copy.wait_recv()
    reg_k = jnp.concatenate([pool[0, 0].astype(F32), pool[1, 0].astype(F32)], axis=0).astype(BF16)
    reg_v = jnp.concatenate([pool[0, 1].astype(F32), pool[1, 1].astype(F32)], axis=0).astype(BF16)

    def bias(rep, relative, start):
        row = lax.broadcasted_iota(jnp.int32, rep.shape, 0)
        key_off = row // CELLS * WIN + row % WIN + relative * WIN
        usable = (key_off >= start - WIN) & (key_off < start + 2 * WIN) & (rep > 0.5)
        half = jnp.where(usable, 0.0, MASKED)
        return jnp.concatenate([half, half], axis=1)

    def partial_stats(keys, values, bdq, bdg, add):
        s = dot(keys, bdq, NT) + add
        dp = dot(values, bdg, NT)
        top = jnp.maximum(jnp.max(s, axis=0, keepdims=True), FLOOR)
        e = jnp.exp(s - top)
        return e, dp, (top, jnp.sum(e, axis=0, keepdims=True))

    def merged(x, y):
        top = jnp.maximum(x[0], y[0])
        fx = jnp.exp(x[0] - top)
        fy = jnp.exp(y[0] - top)
        inverse = 1.0 / (x[1] * fx + y[1] * fy)
        return fx * inverse, fy * inverse

    def probabilities(e, dp, alpha):
        p = e * alpha
        low = p.astype(BF16)
        return p, low, jnp.sum(low.astype(F32) * dp, axis=0, keepdims=True)

    def score_grads(p, dp, delta):
        return (p * (dp - delta)).astype(BF16)

    def rows_of(first, blocks):
        start = first * CELLS
        if not isinstance(start, int):
            start = pl.multiple_of(start, CELLS)
        return pl.ds(start, blocks * CELLS)

    def add_key_grads(a, first, end, p, ds, bdq, bdg, regs):
        rows = (end - first) * CELLS
        dv = dot(p, bdg)
        dk = dot(ds, bdq)
        dv_s[a, first * CELLS : end * CELLS, :] += dv[:rows]
        dk_s[a, first * CELLS : end * CELLS, :] += dk[:rows]
        if regs:
            rv_s[...] += dv[rows:]
            rk_s[...] += dk[rows:]

    def diag_pair(q, g):
        bdq = block_diag(q.reshape(CELLS, 256) * jnp.asarray(SCALE, BF16))
        return bdq, block_diag(g.reshape(CELLS, 256))

    def local_q(a, block):
        return diag_pair(q_in[a, :, block], g_in[a, :, block])

    def local_keys(a, first, end):
        keys = jnp.concatenate([kb[a, first * CELLS : end * CELLS, :], reg_k], axis=0)
        values = jnp.concatenate([vb[a, first * CELLS : end * CELLS, :], reg_v], axis=0)
        return keys, values

    def local_stats(a, block, first, end):
        keys, values = local_keys(a, first, end)
        bdq, bdg = local_q(a, block)
        rep = mrep[a, first * CELLS : end * CELLS, :]
        add = jnp.concatenate(
            [bias(rep, first - block, off_ref[a, block]), jnp.zeros((2 * REG_DEV, 256), F32)], axis=0
        )
        e, dp, stats = partial_stats(keys, values, bdq, bdg, add)
        return keys, bdq, bdg, e, dp, stats

    def edge_stats(a, carry):
        for i, (block, first, end, side, _, _, _) in enumerate(EDGE):
            rows = (end - first) * CELLS + 2 * REG_DEV
            _, _, _, e, dp, stats = local_stats(a, block, first, end)
            e_s[a, i, :rows] = e
            p_s[a, i, :rows] = dp
            slot = i % 2
            for r in range(2):
                own_st[side, a, slot, r : r + 1] = stats[r]
            st_out[side, a, slot, 0:1] = stats[0] + jnp.log(stats[1])
            st_out[side, a, slot, 1:2] = probabilities(e, dp, 1.0 / stats[1])[2]
        return carry

    def middle(a, carry):
        keys, bdq, bdg, e, dp, stats = local_stats(a, 2, 0, NB)
        p, low, delta = probabilities(e, dp, 1.0 / stats[1])
        ds = score_grads(p, dp, delta)
        add_key_grads(a, 0, NB, low, ds, bdq, bdg, True)
        dq = diag_rows(dot(ds, keys, TN)) * SCALE
        o_q[a, :, 2] = dq.reshape(WIN, WIN, 256).astype(BF16)
        return carry

    def foreign_keys(side):
        mask_copy(1 - side).wait_recv()
        for kind in range(2):
            kv_copy(1 - side, kind).wait_recv()

        def body(a, carry):
            mask64 = mask_rows(fmask[side, pl.ds(pl.multiple_of(a * WIN, WIN), WIN), :])
            for slot in range(2):
                frep[slot * CELLS : (slot + 1) * CELLS, :] = mask_cells(mask64, slot + (3 if side == 0 else 0))
            for i, (block, first, end, edge_side, low, high, relative) in enumerate(EDGE):
                if edge_side != side:
                    continue
                rows = (end - first) * CELLS + 2 * REG_DEV
                far_k = jnp.concatenate(
                    [fk[side, a, :, slot].reshape(CELLS, 256) for slot in range(low, high)], axis=0
                )
                far_v = jnp.concatenate(
                    [fv[side, a, :, slot].reshape(CELLS, 256) for slot in range(low, high)], axis=0
                )
                keys, _ = local_keys(a, first, end)
                bdq, bdg = local_q(a, block)
                add = bias(frep[low * CELLS : high * CELLS, :], relative - block, off_ref[a, block])
                far_e, far_dp, far = partial_stats(far_k, far_v, bdq, bdg, add)
                near = tuple(own_st[side, a, i % 2, r : r + 1] for r in range(2))
                alpha, far_alpha = merged(near, far)
                dp = p_s[a, i, :rows]
                p, low_p, share = probabilities(e_s[a, i, :rows], dp, alpha)
                far_p, _, far_share = probabilities(far_e, far_dp, far_alpha)
                delta = share + far_share
                ds = score_grads(p, dp, delta)
                far_ds = score_grads(far_p, far_dp, delta)
                dq = diag_rows(dot(ds, keys, TN) + dot(far_ds, far_k, TN)) * SCALE
                add_key_grads(a, first, end, low_p, ds, bdq, bdg, True)
                o_q[a, :, block] = dq.reshape(WIN, WIN, 256).astype(BF16)
            return carry

        lax.fori_loop(0, NA, body, 0)

    def far_slot(side, blocks):
        return blocks - 1 + side * (3 - 2 * blocks)

    def row0_arrived(side):
        offset_copy(1 - side).wait_recv()
        st_copy(1 - side).wait_recv()
        for kind in range(2):
            qg_copy(1 - side, 0, kind).wait_recv()

    def row1_arrived(side, blocks):
        for kind in range(2):
            one_copy(1 - side, far_slot(side, blocks), kind).wait_recv()

    def far_weights(side, a, blocks):
        slot = far_slot(side, blocks)
        first = side * (NB - blocks)
        relative = jnp.where(side == 0, blocks - 3, 7 - blocks)
        cells = rows_of(first, blocks)
        bdq, bdg = diag_pair(fq[side, a, :, slot], fg[side, a, :, slot])
        top = st_in[side, a, slot, 0:1]
        theirs = (top, jnp.ones_like(top))
        here = (off_row == a) & (off_col == slot + 3 * (1 - side))
        start = jnp.sum(
            jnp.sum(jnp.where(here, far_off[side].astype(F32), 0.0), axis=1, keepdims=True),
            axis=0, keepdims=True,
        ).astype(jnp.int32)
        add = bias(mrep[a, cells, :], first - relative, start)
        e, dp, stats = partial_stats(kb[a, cells, :], vb[a, cells, :], bdq, bdg, add)
        alpha, their_alpha = merged(stats, theirs)
        p, low, share = probabilities(e, dp, alpha)
        ds = score_grads(p, dp, share + their_alpha * st_in[side, a, slot, 1:2])
        return cells, bdq, bdg, (low, ds)

    def add_far(a, unit):
        cells, bdq, bdg, (p, ds) = unit
        dv_s[a, cells, :] += dot(p, bdg)
        dk_s[a, cells, :] += dot(ds, bdq)

    def one_side(side, a):
        @pl.when(a == 0)
        def _():
            row0_arrived(side)

        for blocks in (2, 1):
            @pl.when(a == 1)
            def _():
                row1_arrived(side, blocks)

            add_far(a, far_weights(side, a, blocks))

    def both_sides(a):
        @pl.when(a == 0)
        def _():
            for side in range(2):
                row0_arrived(side)

        @pl.when(a == 1)
        def _():
            for side in range(2):
                for blocks in (2, 1):
                    row1_arrived(side, blocks)

        units = [far_weights(side, a, blocks) for blocks in (2, 1) for side in range(2)]
        for unit in units:
            add_far(a, unit)

    def spread(a, low, high):
        for b in range(low, high):
            mine = row8 == reg_ref[a, b]
            rep = mrep[a, b * CELLS : (b + 1) * CELLS, :]
            rep2 = jnp.concatenate([rep, rep], axis=1)
            for own, total, out in ((rrecv[0], dk_s, o_k), (rrecv[1], dv_s, o_v)):
                row = jnp.sum(jnp.where(mine, own, 0.0), axis=0, keepdims=True)
                cells = total[a, b * CELLS : (b + 1) * CELLS, :] + rep2 * row
                out[a, :, b] = cells.reshape(WIN, WIN, 256).astype(BF16)

    lax.fori_loop(0, NA, edge_stats, 0)
    for copy in later(1):
        copy.start()

    @pl.when(jnp.logical_not(first_tile))
    def _():
        for copy in later(0):
            copy.start()

    lax.fori_loop(0, NA, middle, 0)

    @pl.when(first_tile)
    def _():
        pl.semaphore_wait(late, 1)
        for copy in early(0) + later(0):
            copy.start()

    reg_copy = pltpu.make_async_remote_copy(
        rsend, rrecv, lat_ss.at[1], lat_rs.at[1], device_id={"lat": peer}, device_id_type=MESH
    )
    foreign_keys(1)

    def left_keys():
        foreign_keys(0)
        rsend[0] = rk_s[REG_DEV:, :]
        rsend[1] = rv_s[REG_DEV:, :]
        reg_copy.start()

    def registers_done():
        reg_copy.wait_recv()
        rrecv[0] = (rk_s[:REG_DEV, :] + rrecv[0]) / divisor
        rrecv[1] = (rv_s[:REG_DEV, :] + rrecv[1]) / divisor

    def step(i, carry):
        @pl.when(i == jnp.where(first_tile, 2, 0))
        def _():
            left_keys()

        @pl.when(first_tile & (i != 2))
        def _():
            one_side((i < 2).astype(jnp.int32), jnp.where(i < 2, i, i - 3))

        @pl.when(jnp.logical_not(first_tile) & (i > 0))
        def _():
            both_sides(i - 1)

        @pl.when(i == jnp.where(first_tile, 3, 1))
        def _():
            registers_done()
            spread(0, 0, NB)
            spread(1, 2, 3)

        @pl.when(i == jnp.where(first_tile, 3, 2))
        def _():
            spread(1, 3, NB)

        return carry

    lax.fori_loop(0, jnp.where(first_tile, 5, 3), step, 0)
    spread(1, 0, 2)
    for side in range(2):
        for copy in early(side) + later(side):
            copy.wait_send()
    pool_copy.wait_send()
    reg_copy.wait_send()


def store(a_in, b_in, c_in, a_out, b_out, c_out, sem):
    pairs = ((a_in, a_out), (b_in, b_out), (c_in, c_out))
    copies = [pltpu.make_async_copy(src, dst, sem.at[i]) for i, (src, dst) in enumerate(pairs)]
    for copy in copies:
        copy.start()
    for copy in copies:
        copy.wait()


def local(queries, keys, values, grad_out, key_mask, offsets, regions):
    shape = queries.shape
    grid = (NA, WIN, NB, WIN, 256)
    edge = (2, NA, WIN, 2, WIN, 256)
    hbm_spec = pl.BlockSpec(memory_space=pltpu.HBM)
    vm = pltpu.VMEM
    dma = pltpu.SemaphoreType.DMA
    outs = pl.pallas_call(
        kernel,
        out_shape=[pltpu.VMEM(grid, BF16)] * 3,
        in_specs=[hbm_spec] * 7,
        out_specs=[pl.BlockSpec(memory_space=pltpu.VMEM)] * 3,
        scratch_shapes=[vm(grid, BF16)] * 4
        + [vm((NA, NB * CELLS, 256), BF16)] * 2
        + [vm((NA, NB * CELLS, 128), F32), vm((2 * CELLS, 128), F32)]
        + [vm(edge, BF16)] * 4
        + [vm((2,) + key_mask.shape, jnp.int32)]
        + [vm((NA, 4, 4 * CELLS + 2 * REG_DEV, 256), F32)] * 2
        + [vm((NA, NB * CELLS, 256), F32)] * 2
        + [vm((2 * REG_DEV, 256), F32)] * 2
        + [vm((2, 2, REG_DEV, 256), BF16)]
        + [vm((2, REG_DEV, 256), F32)] * 2
        + [vm((2, NA, 2, 8, 256), F32)]
        + [vm((2, NA, 2, 2, 256), F32)] * 2
        + [vm((2,) + offsets.shape, jnp.int32)]
        + [vm(key_mask.shape, jnp.int32)]
        + [pltpu.SMEM(offsets.shape, jnp.int32)] * 2
        + [dma((7,))]
        + [dma((2, 2))] * 2
        + [dma((2, NA, 2))] * 2
        + [dma((2,))] * 6
        + [dma((2, 2, 2))] * 2
        + [dma((2,))] * 2
        + [pltpu.SemaphoreType.REGULAR] * 4,
        compiler_params=pltpu.CompilerParams(
            collective_id=0, has_side_effects=True, vmem_limit_bytes=VMEM_BYTES
        ),
        cost_estimate=pl.CostEstimate(flops=2200000000, bytes_accessed=2300000, transcendentals=860000),
    )(
        *(x.reshape(grid) for x in (queries, keys, values, grad_out)), key_mask, offsets, regions
    )
    outs = pl.pallas_call(
        store,
        out_shape=[jax.ShapeDtypeStruct(grid, BF16)] * 3,
        in_specs=[pl.BlockSpec(memory_space=pl.ANY)] * 3,
        out_specs=[hbm_spec] * 3,
        scratch_shapes=[dma((3,))],
        compiler_params=pltpu.CompilerParams(vmem_limit_bytes=1024 * 1024),
    )(*outs)
    return tuple(x.reshape(shape) for x in outs)


def solution(mesh):
    tile = P("lat", "lon", "head")
    cells = P("lat", "lon")
    return jax.shard_map(
        local, mesh=mesh, in_specs=(tile,) * 4 + (cells,) * 3, out_specs=(tile,) * 3, check_vma=False
    )
```

```python
import jax
import jax.numpy as jnp
from jax import lax
from jax.experimental import pallas as pl
from jax.experimental.pallas import tpu as pltpu
from jax.sharding import PartitionSpec as P

HS = 64
WIN = 8
CELLS = WIN * WIN
REG_DEV = 8
NA = 2
NB = 5
VMEM_BYTES = 56 * 1024 * 1024
MASKED = -1.0e30
FLOOR = -1.0e29
SCALE = HS ** (-0.5)
MESH = pl.DeviceIdType.MESH
NT = (((1,), (1,)), ((), ()))
TN = (((0,), (0,)), ((), ()))
F32 = jnp.float32
BF16 = jnp.bfloat16

EDGE = (
    (0, 0, 3, 0, 0, 2, -2), (1, 0, 4, 0, 1, 2, -1),
    (3, 1, 5, 1, 0, 1, 5), (4, 2, 5, 1, 0, 2, 5),
)


def dot(a, b, dims=(((1,), (0,)), ((), ()))):
    return lax.dot_general(a, b, dims, preferred_element_type=F32)


def kernel(
    q_hbm, k_hbm, v_hbm, g_hbm, mask_hbm, off_hbm, reg_hbm,
    o_q, o_k, o_v,
    q_in, k_in, v_in, g_in, kb, vb, mrep, frep,
    fk, fv, fq, fg, fmask, e_s, p_s, dk_s, dv_s, rk_s, rv_s,
    pool, rsend, rrecv, own_st, st_out, st_in, far_off,
    mask_ref, off_ref, reg_ref,
    in_sem, kv_ss, kv_rs, qg_ss, qg_rs, mk_ss, mk_rs, st_ss, st_rs, of_ss, of_rs, one_ss, one_rs, lat_ss, lat_rs, late, go, chain, peer_in,
):
    count = lax.axis_size("lon")
    me = lax.axis_index("lon")
    right = lax.rem(me + 1, count)
    left = lax.rem(me + count - 1, count)
    peer = 1 - lax.axis_index("lat")
    sides = ({"lon": left}, {"lon": right})
    first_tile = me == 0
    last_tile = me == count - 1

    before_last = me == count - 2

    barrier = pltpu.get_barrier_semaphore()
    pl.semaphore_signal(barrier, inc=1, device_id=sides[0], device_id_type=MESH)

    @pl.when(me < count - 2)
    def _():
        pl.semaphore_signal(barrier, inc=1, device_id=sides[1], device_id_type=MESH)

    @pl.when(jnp.logical_not(last_tile))
    def _():
        pl.semaphore_signal(barrier, inc=1, device_id={"lat": peer}, device_id_type=MESH)

    pl.semaphore_wait(barrier, jnp.where(last_tile, 1, jnp.where(first_tile, 2, 3)))

    @pl.when(last_tile)
    def _():
        pl.semaphore_signal(late, inc=1, device_id=sides[1], device_id_type=MESH)

    @pl.when(before_last)
    def _():
        pl.semaphore_signal(chain, inc=1, device_id={"lat": peer}, device_id_type=MESH)
        pl.semaphore_signal(go, inc=1, device_id=sides[1], device_id_type=MESH)

    loads = [
        pltpu.make_async_copy(src, dst, in_sem.at[i])
        for i, (src, dst) in enumerate((
            (mask_hbm, mask_ref), (off_hbm, off_ref), (reg_hbm, reg_ref),
            (k_hbm, k_in), (v_hbm, v_in), (q_hbm, q_in), (g_hbm, g_in),
        ))
    ]

    def edge_blocks(side):
        return pl.ds(3 * side, 2)

    def remote(src, dst, ss, rs, side):
        return pltpu.make_async_remote_copy(
            src, dst, ss, rs, device_id={"lon": jnp.where(side == 0, left, right)}, device_id_type=MESH
        )

    def mask_copy(side):
        return remote(mask_hbm, fmask.at[1 - side], mk_ss.at[side], mk_rs.at[1 - side], side)

    def kv_copy(side, kind):
        src = (k_hbm, v_hbm)[kind].at[:, :, edge_blocks(side)]
        dst = (fk, fv)[kind].at[1 - side]
        return remote(src, dst, kv_ss.at[side, kind], kv_rs.at[1 - side, kind], side)

    def qg_copy(side, a, kind):
        src = (q_hbm, g_hbm)[kind].at[a, :, edge_blocks(side)]
        dst = (fq, fg)[kind].at[1 - side, a]
        return remote(src, dst, qg_ss.at[side, a, kind], qg_rs.at[1 - side, a, kind], side)

    def offset_copy(side):
        return remote(off_hbm, far_off.at[1 - side], of_ss.at[side], of_rs.at[1 - side], side)

    def one_copy(side, slot, kind):
        src = (q_hbm, g_hbm)[kind].at[1, :, 3 * side + slot]
        dst = (fq, fg)[kind].at[1 - side, 1, :, slot]
        return remote(src, dst, one_ss.at[side, slot, kind], one_rs.at[1 - side, slot, kind], side)

    def st_copy(side):
        return remote(st_out.at[side], st_in.at[1 - side], st_ss.at[side], st_rs.at[1 - side], side)

    def early(side):
        copies = [kv_copy(side, kind) for kind in range(2)] + [mask_copy(side), offset_copy(side)]
        return copies + [qg_copy(side, 0, kind) for kind in range(2)]

    def later(side):
        outer = side
        slots = (outer, 1 - outer)
        return [st_copy(side)] + [one_copy(side, slot, kind) for slot in slots for kind in range(2)]

    for copy in early(1) + loads:
        copy.start()

    @pl.when(jnp.logical_not(first_tile | last_tile))
    def _():
        for copy in early(0):
            copy.start()

    @pl.when(before_last)
    def _():
        pl.semaphore_wait(chain, 1)
        pl.semaphore_signal(peer_in, inc=1, device_id=sides[1], device_id_type=MESH)

    lane_head = lax.broadcasted_iota(jnp.int32, (CELLS, 4 * HS), 1) // HS
    head_mask = [(lane_head == h).astype(F32).astype(BF16) for h in range(4)]
    low_half = lax.broadcasted_iota(jnp.int32, (CELLS, 128), 1) < HS

    def block_diag(x):
        return jnp.concatenate([x * head_mask[h] for h in range(4)], axis=0)

    def diag_rows(full):
        return jnp.concatenate(
            [
                jnp.where(low_half, full[0:64, 0:128], full[64:128, 0:128]),
                jnp.where(low_half, full[128:192, 128:256], full[192:256, 128:256]),
            ],
            axis=1,
        )

    for copy in loads:
        copy.wait()

    cell_t = lax.broadcasted_iota(jnp.int32, (CELLS, NB * WIN), 0) % WIN
    lane = lax.broadcasted_iota(jnp.int32, (CELLS, NB * WIN), 1)
    off_row = lax.broadcasted_iota(jnp.int32, (NA, NB), 0)
    off_col = lax.broadcasted_iota(jnp.int32, (NA, NB), 1)
    row8 = lax.broadcasted_iota(jnp.int32, (REG_DEV, 256), 0)

    def mask_rows(mask8):
        mask8 = mask8.astype(F32)
        return jnp.broadcast_to(mask8[:, None, :], (WIN, WIN, NB * WIN)).reshape(CELLS, NB * WIN)

    def mask_cells(mask64, b):
        column = jnp.sum(jnp.where(lane == cell_t + b * WIN, mask64, 0.0), axis=1, keepdims=True)
        return jnp.broadcast_to(column, (CELLS, 128))

    pk = jnp.zeros((REG_DEV, 256), F32)
    pv = jnp.zeros((REG_DEV, 256), F32)
    cnt = jnp.zeros((REG_DEV, 256), F32)
    for a in range(NA):
        mask64 = mask_rows(mask_ref[a * WIN : (a + 1) * WIN, :])
        for b in range(NB):
            rep = mask_cells(mask64, b)
            mrep[a, b * CELLS : (b + 1) * CELLS, :] = rep
            rep2 = jnp.concatenate([rep, rep], axis=1)
            kx = k_in[a, :, b].reshape(CELLS, 256)
            vx = v_in[a, :, b].reshape(CELLS, 256)
            kb[a, b * CELLS : (b + 1) * CELLS, :] = kx
            vb[a, b * CELLS : (b + 1) * CELLS, :] = vx
            mine = row8 == reg_ref[a, b]
            pk = pk + jnp.where(mine, jnp.sum(kx.astype(F32) * rep2, axis=0, keepdims=True), 0.0)
            pv = pv + jnp.where(mine, jnp.sum(vx.astype(F32) * rep2, axis=0, keepdims=True), 0.0)
            cnt = cnt + jnp.where(mine, jnp.sum(rep2, axis=0, keepdims=True), 0.0)
    divisor = jnp.maximum(cnt, 1.0)
    pool[0, 0] = (pk / divisor).astype(BF16)
    pool[0, 1] = (pv / divisor).astype(BF16)
    pool_copy = pltpu.make_async_remote_copy(
        pool.at[0], pool.at[1], lat_ss.at[0], lat_rs.at[0], device_id={"lat": peer}, device_id_type=MESH
    )

    @pl.when(last_tile)
    def _():
        pl.semaphore_wait(go, 1)
        for copy in early(0):
            copy.start()
        pl.semaphore_wait(peer_in, 1)

    pool_copy.start()
    dk_s[...] = jnp.zeros_like(dk_s)
    dv_s[...] = jnp.zeros_like(dv_s)
    rk_s[...] = jnp.zeros_like(rk_s)
    rv_s[...] = jnp.zeros_like(rv_s)
    pool_copy.wait_recv()
    reg_k = jnp.concatenate([pool[0, 0].astype(F32), pool[1, 0].astype(F32)], axis=0).astype(BF16)
    reg_v = jnp.concatenate([pool[0, 1].astype(F32), pool[1, 1].astype(F32)], axis=0).astype(BF16)

    def bias(rep, relative, start):
        row = lax.broadcasted_iota(jnp.int32, rep.shape, 0)
        key_off = row // CELLS * WIN + row % WIN + relative * WIN
        usable = (key_off >= start - WIN) & (key_off < start + 2 * WIN) & (rep > 0.5)
        half = jnp.where(usable, 0.0, MASKED)
        return jnp.concatenate([half, half], axis=1)

    def partial_stats(keys, values, bdq, bdg, add):
        s = dot(keys, bdq, NT) + add
        dp = dot(values, bdg, NT)
        top = jnp.maximum(jnp.max(s, axis=0, keepdims=True), FLOOR)
        e = jnp.exp(s - top)
        return e, dp, (top, jnp.sum(e, axis=0, keepdims=True))

    def merged(x, y):
        top = jnp.maximum(x[0], y[0])
        fx = jnp.exp(x[0] - top)
        fy = jnp.exp(y[0] - top)
        inverse = 1.0 / (x[1] * fx + y[1] * fy)
        return fx * inverse, fy * inverse

    def probabilities(e, dp, alpha):
        p = e * alpha
        low = p.astype(BF16)
        return p, low, jnp.sum(low.astype(F32) * dp, axis=0, keepdims=True)

    def score_grads(p, dp, delta):
        return (p * (dp - delta)).astype(BF16)

    def rows_of(first, blocks):
        start = first * CELLS
        if not isinstance(start, int):
            start = pl.multiple_of(start, CELLS)
        return pl.ds(start, blocks * CELLS)

    def add_key_grads(a, first, end, p, ds, bdq, bdg, regs):
        rows = (end - first) * CELLS
        dv = dot(p, bdg)
        dk = dot(ds, bdq)
        dv_s[a, first * CELLS : end * CELLS, :] += dv[:rows]
        dk_s[a, first * CELLS : end * CELLS, :] += dk[:rows]
        if regs:
            rv_s[...] += dv[rows:]
            rk_s[...] += dk[rows:]

    def diag_pair(q, g):
        bdq = block_diag(q.reshape(CELLS, 256) * jnp.asarray(SCALE, BF16))
        return bdq, block_diag(g.reshape(CELLS, 256))

    def local_q(a, block):
        return diag_pair(q_in[a, :, block], g_in[a, :, block])

    def local_keys(a, first, end):
        keys = jnp.concatenate([kb[a, first * CELLS : end * CELLS, :], reg_k], axis=0)
        values = jnp.concatenate([vb[a, first * CELLS : end * CELLS, :], reg_v], axis=0)
        return keys, values

    def local_stats(a, block, first, end):
        keys, values = local_keys(a, first, end)
        bdq, bdg = local_q(a, block)
        rep = mrep[a, first * CELLS : end * CELLS, :]
        add = jnp.concatenate(
            [bias(rep, first - block, off_ref[a, block]), jnp.zeros((2 * REG_DEV, 256), F32)], axis=0
        )
        e, dp, stats = partial_stats(keys, values, bdq, bdg, add)
        return keys, bdq, bdg, e, dp, stats

    def edge_stats(a, carry):
        for i, (block, first, end, side, _, _, _) in enumerate(EDGE):
            rows = (end - first) * CELLS + 2 * REG_DEV
            _, _, _, e, dp, stats = local_stats(a, block, first, end)
            e_s[a, i, :rows] = e
            p_s[a, i, :rows] = dp
            slot = i % 2
            for r in range(2):
                own_st[side, a, slot, r : r + 1] = stats[r]
            st_out[side, a, slot, 0:1] = stats[0] + jnp.log(stats[1])
            st_out[side, a, slot, 1:2] = probabilities(e, dp, 1.0 / stats[1])[2]
        return carry

    def middle(a, carry):
        keys, bdq, bdg, e, dp, stats = local_stats(a, 2, 0, NB)
        p, low, delta = probabilities(e, dp, 1.0 / stats[1])
        ds = score_grads(p, dp, delta)
        add_key_grads(a, 0, NB, low, ds, bdq, bdg, True)
        dq = diag_rows(dot(ds, keys, TN)) * SCALE
        o_q[a, :, 2] = dq.reshape(WIN, WIN, 256).astype(BF16)
        return carry

    def foreign_keys(side):
        mask_copy(1 - side).wait_recv()
        for kind in range(2):
            kv_copy(1 - side, kind).wait_recv()

        def body(a, carry):
            mask64 = mask_rows(fmask[side, pl.ds(pl.multiple_of(a * WIN, WIN), WIN), :])
            for slot in range(2):
                frep[slot * CELLS : (slot + 1) * CELLS, :] = mask_cells(mask64, slot + (3 if side == 0 else 0))
            for i, (block, first, end, edge_side, low, high, relative) in enumerate(EDGE):
                if edge_side != side:
                    continue
                rows = (end - first) * CELLS + 2 * REG_DEV
                far_k = jnp.concatenate(
                    [fk[side, a, :, slot].reshape(CELLS, 256) for slot in range(low, high)], axis=0
                )
                far_v = jnp.concatenate(
                    [fv[side, a, :, slot].reshape(CELLS, 256) for slot in range(low, high)], axis=0
                )
                keys, _ = local_keys(a, first, end)
                bdq, bdg = local_q(a, block)
                add = bias(frep[low * CELLS : high * CELLS, :], relative - block, off_ref[a, block])
                far_e, far_dp, far = partial_stats(far_k, far_v, bdq, bdg, add)
                near = tuple(own_st[side, a, i % 2, r : r + 1] for r in range(2))
                alpha, far_alpha = merged(near, far)
                dp = p_s[a, i, :rows]
                p, low_p, share = probabilities(e_s[a, i, :rows], dp, alpha)
                far_p, _, far_share = probabilities(far_e, far_dp, far_alpha)
                delta = share + far_share
                ds = score_grads(p, dp, delta)
                far_ds = score_grads(far_p, far_dp, delta)
                dq = diag_rows(dot(ds, keys, TN) + dot(far_ds, far_k, TN)) * SCALE
                add_key_grads(a, first, end, low_p, ds, bdq, bdg, True)
                o_q[a, :, block] = dq.reshape(WIN, WIN, 256).astype(BF16)
            return carry

        lax.fori_loop(0, NA, body, 0)

    def far_slot(side, blocks):
        return blocks - 1 + side * (3 - 2 * blocks)

    def row0_arrived(side):
        offset_copy(1 - side).wait_recv()
        st_copy(1 - side).wait_recv()
        for kind in range(2):
            qg_copy(1 - side, 0, kind).wait_recv()

    def row1_arrived(side, blocks):
        for kind in range(2):
            one_copy(1 - side, far_slot(side, blocks), kind).wait_recv()

    def far_weights(side, a, blocks):
        slot = far_slot(side, blocks)
        first = side * (NB - blocks)
        relative = jnp.where(side == 0, blocks - 3, 7 - blocks)
        cells = rows_of(first, blocks)
        bdq, bdg = diag_pair(fq[side, a, :, slot], fg[side, a, :, slot])
        top = st_in[side, a, slot, 0:1]
        theirs = (top, jnp.ones_like(top))
        here = (off_row == a) & (off_col == slot + 3 * (1 - side))
        start = jnp.sum(
            jnp.sum(jnp.where(here, far_off[side].astype(F32), 0.0), axis=1, keepdims=True),
            axis=0, keepdims=True,
        ).astype(jnp.int32)
        add = bias(mrep[a, cells, :], first - relative, start)
        e, dp, stats = partial_stats(kb[a, cells, :], vb[a, cells, :], bdq, bdg, add)
        alpha, their_alpha = merged(stats, theirs)
        p, low, share = probabilities(e, dp, alpha)
        ds = score_grads(p, dp, share + their_alpha * st_in[side, a, slot, 1:2])
        return cells, bdq, bdg, (low, ds)

    def add_far(a, unit):
        cells, bdq, bdg, (p, ds) = unit
        dv_s[a, cells, :] += dot(p, bdg)
        dk_s[a, cells, :] += dot(ds, bdq)

    def one_side(side, a):
        @pl.when(a == 0)
        def _():
            row0_arrived(side)

        for blocks in (2, 1):
            @pl.when(a == 1)
            def _():
                row1_arrived(side, blocks)

            add_far(a, far_weights(side, a, blocks))

    def both_sides(a):
        @pl.when(a == 0)
        def _():
            for side in range(2):
                row0_arrived(side)

        @pl.when(a == 1)
        def _():
            for side in range(2):
                for blocks in (2, 1):
                    row1_arrived(side, blocks)

        units = [far_weights(side, a, blocks) for blocks in (2, 1) for side in range(2)]
        for unit in units:
            add_far(a, unit)

    def spread(a, low, high):
        for b in range(low, high):
            mine = row8 == reg_ref[a, b]
            rep = mrep[a, b * CELLS : (b + 1) * CELLS, :]
            rep2 = jnp.concatenate([rep, rep], axis=1)
            for own, total, out in ((rrecv[0], dk_s, o_k), (rrecv[1], dv_s, o_v)):
                row = jnp.sum(jnp.where(mine, own, 0.0), axis=0, keepdims=True)
                cells = total[a, b * CELLS : (b + 1) * CELLS, :] + rep2 * row
                out[a, :, b] = cells.reshape(WIN, WIN, 256).astype(BF16)

    lax.fori_loop(0, NA, edge_stats, 0)
    for copy in later(1):
        copy.start()

    @pl.when(jnp.logical_not(first_tile))
    def _():
        for copy in later(0):
            copy.start()

    lax.fori_loop(0, NA, middle, 0)

    @pl.when(first_tile)
    def _():
        pl.semaphore_wait(late, 1)
        for copy in early(0) + later(0):
            copy.start()

    reg_copy = pltpu.make_async_remote_copy(
        rsend, rrecv, lat_ss.at[1], lat_rs.at[1], device_id={"lat": peer}, device_id_type=MESH
    )
    foreign_keys(1)

    def left_keys():
        foreign_keys(0)
        rsend[0] = rk_s[REG_DEV:, :]
        rsend[1] = rv_s[REG_DEV:, :]
        reg_copy.start()

    def registers_done():
        reg_copy.wait_recv()
        rrecv[0] = (rk_s[:REG_DEV, :] + rrecv[0]) / divisor
        rrecv[1] = (rv_s[:REG_DEV, :] + rrecv[1]) / divisor

    def step(i, carry):
        @pl.when(i == jnp.where(first_tile, 2, 0))
        def _():
            left_keys()

        @pl.when(first_tile & (i != 2))
        def _():
            one_side((i < 2).astype(jnp.int32), jnp.where(i < 2, i, i - 3))

        @pl.when(jnp.logical_not(first_tile) & (i > 0))
        def _():
            both_sides(i - 1)

        @pl.when(i == jnp.where(first_tile, 3, 1))
        def _():
            registers_done()
            spread(0, 0, NB)
            spread(1, 2, 3)

        @pl.when(i == jnp.where(first_tile, 3, 2))
        def _():
            spread(1, 3, NB)

        return carry

    lax.fori_loop(0, jnp.where(first_tile, 4, 3), step, 0)

    @pl.when(first_tile)
    def _():
        for blocks in (2, 1):
            row1_arrived(0, blocks)
        units = [far_weights(0, 1, blocks) for blocks in (2, 1)]
        for unit in units:
            add_far(1, unit)

    spread(1, 0, 2)
    for side in range(2):
        for copy in early(side) + later(side):
            copy.wait_send()
    pool_copy.wait_send()
    reg_copy.wait_send()


def store(a_in, b_in, c_in, a_out, b_out, c_out, sem):
    pairs = ((a_in, a_out), (b_in, b_out), (c_in, c_out))
    copies = [pltpu.make_async_copy(src, dst, sem.at[i]) for i, (src, dst) in enumerate(pairs)]
    for copy in copies:
        copy.start()
    for copy in copies:
        copy.wait()


def local(queries, keys, values, grad_out, key_mask, offsets, regions):
    shape = queries.shape
    grid = (NA, WIN, NB, WIN, 256)
    edge = (2, NA, WIN, 2, WIN, 256)
    hbm_spec = pl.BlockSpec(memory_space=pltpu.HBM)
    vm = pltpu.VMEM
    dma = pltpu.SemaphoreType.DMA
    outs = pl.pallas_call(
        kernel,
        out_shape=[pltpu.VMEM(grid, BF16)] * 3,
        in_specs=[hbm_spec] * 7,
        out_specs=[pl.BlockSpec(memory_space=pltpu.VMEM)] * 3,
        scratch_shapes=[vm(grid, BF16)] * 4
        + [vm((NA, NB * CELLS, 256), BF16)] * 2
        + [vm((NA, NB * CELLS, 128), F32), vm((2 * CELLS, 128), F32)]
        + [vm(edge, BF16)] * 4
        + [vm((2,) + key_mask.shape, jnp.int32)]
        + [vm((NA, 4, 4 * CELLS + 2 * REG_DEV, 256), F32)] * 2
        + [vm((NA, NB * CELLS, 256), F32)] * 2
        + [vm((2 * REG_DEV, 256), F32)] * 2
        + [vm((2, 2, REG_DEV, 256), BF16)]
        + [vm((2, REG_DEV, 256), F32)] * 2
        + [vm((2, NA, 2, 8, 256), F32)]
        + [vm((2, NA, 2, 2, 256), F32)] * 2
        + [vm((2,) + offsets.shape, jnp.int32)]
        + [vm(key_mask.shape, jnp.int32)]
        + [pltpu.SMEM(offsets.shape, jnp.int32)] * 2
        + [dma((7,))]
        + [dma((2, 2))] * 2
        + [dma((2, NA, 2))] * 2
        + [dma((2,))] * 6
        + [dma((2, 2, 2))] * 2
        + [dma((2,))] * 2
        + [pltpu.SemaphoreType.REGULAR] * 4,
        compiler_params=pltpu.CompilerParams(
            collective_id=0, has_side_effects=True, vmem_limit_bytes=VMEM_BYTES
        ),
        cost_estimate=pl.CostEstimate(flops=2200000000, bytes_accessed=2300000, transcendentals=860000),
    )(
        *(x.reshape(grid) for x in (queries, keys, values, grad_out)), key_mask, offsets, regions
    )
    outs = pl.pallas_call(
        store,
        out_shape=[jax.ShapeDtypeStruct(grid, BF16)] * 3,
        in_specs=[pl.BlockSpec(memory_space=pl.ANY)] * 3,
        out_specs=[hbm_spec] * 3,
        scratch_shapes=[dma((3,))],
        compiler_params=pltpu.CompilerParams(vmem_limit_bytes=1024 * 1024),
    )(*outs)
    return tuple(x.reshape(shape) for x in outs)


def solution(mesh):
    tile = P("lat", "lon", "head")
    cells = P("lat", "lon")
    return jax.shard_map(
        local, mesh=mesh, in_specs=(tile,) * 4 + (cells,) * 3, out_specs=(tile,) * 3, check_vma=False
    )
```

```python
import jax
import jax.numpy as jnp
from jax import lax
from jax.experimental import pallas as pl
from jax.experimental.pallas import tpu as pltpu
from jax.sharding import PartitionSpec as P

HS = 64
WIN = 8
CELLS = WIN * WIN
REG_DEV = 8
NA = 2
NB = 5
VMEM_BYTES = 56 * 1024 * 1024
MASKED = -1.0e30
FLOOR = -1.0e29
SCALE = HS ** (-0.5)
MESH = pl.DeviceIdType.MESH
NT = (((1,), (1,)), ((), ()))
TN = (((0,), (0,)), ((), ()))
F32 = jnp.float32
BF16 = jnp.bfloat16

EDGE = (
    (0, 0, 3, 0, 0, 2, -2), (1, 0, 4, 0, 1, 2, -1),
    (3, 1, 5, 1, 0, 1, 5), (4, 2, 5, 1, 0, 2, 5),
)


def dot(a, b, dims=(((1,), (0,)), ((), ()))):
    return lax.dot_general(a, b, dims, preferred_element_type=F32)


def kernel(
    q_hbm, k_hbm, v_hbm, g_hbm, mask_hbm, off_hbm, reg_hbm,
    o_q, o_k, o_v,
    q_in, k_in, v_in, g_in, kb, vb, mrep, frep,
    fk, fv, fq, fg, fmask, e_s, p_s, dk_s, dv_s, rk_s, rv_s,
    pool, rsend, rrecv, own_st, st_out, st_in, far_off,
    mask_ref, off_ref, reg_ref,
    in_sem, kv_ss, kv_rs, qg_ss, qg_rs, mk_ss, mk_rs, st_ss, st_rs, of_ss, of_rs, one_ss, one_rs, lat_ss, lat_rs, late, go, chain, peer_in,
):
    count = lax.axis_size("lon")
    me = lax.axis_index("lon")
    right = lax.rem(me + 1, count)
    left = lax.rem(me + count - 1, count)
    peer = 1 - lax.axis_index("lat")
    sides = ({"lon": left}, {"lon": right})
    first_tile = me == 0
    last_tile = me == count - 1

    before_last = me == count - 2

    barrier = pltpu.get_barrier_semaphore()
    pl.semaphore_signal(barrier, inc=1, device_id=sides[0], device_id_type=MESH)

    @pl.when(me < count - 2)
    def _():
        pl.semaphore_signal(barrier, inc=1, device_id=sides[1], device_id_type=MESH)

    @pl.when(jnp.logical_not(last_tile))
    def _():
        pl.semaphore_signal(barrier, inc=1, device_id={"lat": peer}, device_id_type=MESH)

    pl.semaphore_wait(barrier, jnp.where(last_tile, 1, jnp.where(first_tile, 2, 3)))

    @pl.when(last_tile)
    def _():
        pl.semaphore_signal(late, inc=1, device_id=sides[1], device_id_type=MESH)

    @pl.when(before_last)
    def _():
        pl.semaphore_signal(chain, inc=1, device_id={"lat": peer}, device_id_type=MESH)
        pl.semaphore_signal(go, inc=1, device_id=sides[1], device_id_type=MESH)

    loads = [
        pltpu.make_async_copy(src, dst, in_sem.at[i])
        for i, (src, dst) in enumerate((
            (mask_hbm, mask_ref), (off_hbm, off_ref), (reg_hbm, reg_ref),
            (k_hbm, k_in), (v_hbm, v_in), (q_hbm, q_in), (g_hbm, g_in),
        ))
    ]

    def edge_blocks(side):
        return pl.ds(3 * side, 2)

    def remote(src, dst, ss, rs, side):
        return pltpu.make_async_remote_copy(
            src, dst, ss, rs, device_id={"lon": jnp.where(side == 0, left, right)}, device_id_type=MESH
        )

    def mask_copy(side):
        return remote(mask_hbm, fmask.at[1 - side], mk_ss.at[side], mk_rs.at[1 - side], side)

    def kv_copy(side, kind):
        src = (k_hbm, v_hbm)[kind].at[:, :, edge_blocks(side)]
        dst = (fk, fv)[kind].at[1 - side]
        return remote(src, dst, kv_ss.at[side, kind], kv_rs.at[1 - side, kind], side)

    def qg_copy(side, a, kind):
        src = (q_hbm, g_hbm)[kind].at[a, :, edge_blocks(side)]
        dst = (fq, fg)[kind].at[1 - side, a]
        return remote(src, dst, qg_ss.at[side, a, kind], qg_rs.at[1 - side, a, kind], side)

    def offset_copy(side):
        return remote(off_hbm, far_off.at[1 - side], of_ss.at[side], of_rs.at[1 - side], side)

    def one_copy(side, slot, kind):
        src = (q_hbm, g_hbm)[kind].at[1, :, 3 * side + slot]
        dst = (fq, fg)[kind].at[1 - side, 1, :, slot]
        return remote(src, dst, one_ss.at[side, slot, kind], one_rs.at[1 - side, slot, kind], side)

    def st_copy(side):
        return remote(st_out.at[side], st_in.at[1 - side], st_ss.at[side], st_rs.at[1 - side], side)

    def early(side):
        copies = [kv_copy(side, kind) for kind in range(2)] + [mask_copy(side), offset_copy(side)]
        return copies + [qg_copy(side, 0, kind) for kind in range(2)]

    def later(side):
        outer = side
        slots = (outer, 1 - outer)
        return [st_copy(side)] + [one_copy(side, slot, kind) for slot in slots for kind in range(2)]

    for copy in early(1) + loads:
        copy.start()

    @pl.when(jnp.logical_not(first_tile | last_tile))
    def _():
        for copy in early(0):
            copy.start()

    @pl.when(before_last)
    def _():
        pl.semaphore_wait(chain, 1)
        pl.semaphore_signal(peer_in, inc=1, device_id=sides[1], device_id_type=MESH)

    lane_head = lax.broadcasted_iota(jnp.int32, (CELLS, 4 * HS), 1) // HS
    head_mask = [(lane_head == h).astype(F32).astype(BF16) for h in range(4)]
    low_half = lax.broadcasted_iota(jnp.int32, (CELLS, 128), 1) < HS

    def block_diag(x):
        return jnp.concatenate([x * head_mask[h] for h in range(4)], axis=0)

    def diag_rows(full):
        return jnp.concatenate(
            [
                jnp.where(low_half, full[0:64, 0:128], full[64:128, 0:128]),
                jnp.where(low_half, full[128:192, 128:256], full[192:256, 128:256]),
            ],
            axis=1,
        )

    for copy in loads:
        copy.wait()

    cell_t = lax.broadcasted_iota(jnp.int32, (CELLS, NB * WIN), 0) % WIN
    lane = lax.broadcasted_iota(jnp.int32, (CELLS, NB * WIN), 1)
    off_row = lax.broadcasted_iota(jnp.int32, (NA, NB), 0)
    off_col = lax.broadcasted_iota(jnp.int32, (NA, NB), 1)
    row8 = lax.broadcasted_iota(jnp.int32, (REG_DEV, 256), 0)

    def mask_rows(mask8):
        mask8 = mask8.astype(F32)
        return jnp.broadcast_to(mask8[:, None, :], (WIN, WIN, NB * WIN)).reshape(CELLS, NB * WIN)

    def mask_cells(mask64, b):
        column = jnp.sum(jnp.where(lane == cell_t + b * WIN, mask64, 0.0), axis=1, keepdims=True)
        return jnp.broadcast_to(column, (CELLS, 128))

    pk = jnp.zeros((REG_DEV, 256), F32)
    pv = jnp.zeros((REG_DEV, 256), F32)
    cnt = jnp.zeros((REG_DEV, 256), F32)
    for a in range(NA):
        mask64 = mask_rows(mask_ref[a * WIN : (a + 1) * WIN, :])
        for b in range(NB):
            rep = mask_cells(mask64, b)
            mrep[a, b * CELLS : (b + 1) * CELLS, :] = rep
            rep2 = jnp.concatenate([rep, rep], axis=1)
            kx = k_in[a, :, b].reshape(CELLS, 256)
            vx = v_in[a, :, b].reshape(CELLS, 256)
            kb[a, b * CELLS : (b + 1) * CELLS, :] = kx
            vb[a, b * CELLS : (b + 1) * CELLS, :] = vx
            mine = row8 == reg_ref[a, b]
            pk = pk + jnp.where(mine, jnp.sum(kx.astype(F32) * rep2, axis=0, keepdims=True), 0.0)
            pv = pv + jnp.where(mine, jnp.sum(vx.astype(F32) * rep2, axis=0, keepdims=True), 0.0)
            cnt = cnt + jnp.where(mine, jnp.sum(rep2, axis=0, keepdims=True), 0.0)
    divisor = jnp.maximum(cnt, 1.0)
    pool[0, 0] = (pk / divisor).astype(BF16)
    pool[0, 1] = (pv / divisor).astype(BF16)
    pool_copy = pltpu.make_async_remote_copy(
        pool.at[0], pool.at[1], lat_ss.at[0], lat_rs.at[0], device_id={"lat": peer}, device_id_type=MESH
    )

    @pl.when(last_tile)
    def _():
        pl.semaphore_wait(go, 1)
        for copy in early(0):
            copy.start()
        pl.semaphore_wait(peer_in, 1)

    pool_copy.start()
    dk_s[...] = jnp.zeros_like(dk_s)
    dv_s[...] = jnp.zeros_like(dv_s)
    rk_s[...] = jnp.zeros_like(rk_s)
    rv_s[...] = jnp.zeros_like(rv_s)
    pool_copy.wait_recv()
    reg_k = jnp.concatenate([pool[0, 0].astype(F32), pool[1, 0].astype(F32)], axis=0).astype(BF16)
    reg_v = jnp.concatenate([pool[0, 1].astype(F32), pool[1, 1].astype(F32)], axis=0).astype(BF16)

    def bias(rep, relative, start):
        row = lax.broadcasted_iota(jnp.int32, rep.shape, 0)
        key_off = row // CELLS * WIN + row % WIN + relative * WIN
        usable = (key_off >= start - WIN) & (key_off < start + 2 * WIN) & (rep > 0.5)
        half = jnp.where(usable, 0.0, MASKED)
        return jnp.concatenate([half, half], axis=1)

    def partial_stats(keys, values, bdq, bdg, add):
        s = dot(keys, bdq, NT) + add
        dp = dot(values, bdg, NT)
        top = jnp.maximum(jnp.max(s, axis=0, keepdims=True), FLOOR)
        e = jnp.exp(s - top)
        return e, dp, (top, jnp.sum(e, axis=0, keepdims=True))

    def merged(x, y):
        top = jnp.maximum(x[0], y[0])
        fx = jnp.exp(x[0] - top)
        fy = jnp.exp(y[0] - top)
        inverse = 1.0 / (x[1] * fx + y[1] * fy)
        return fx * inverse, fy * inverse

    def probabilities(e, dp, alpha):
        p = e * alpha
        low = p.astype(BF16)
        return p, low, jnp.sum(low.astype(F32) * dp, axis=0, keepdims=True)

    def score_grads(p, dp, delta):
        return (p * (dp - delta)).astype(BF16)

    def rows_of(first, blocks):
        start = first * CELLS
        if not isinstance(start, int):
            start = pl.multiple_of(start, CELLS)
        return pl.ds(start, blocks * CELLS)

    def add_key_grads(a, first, end, p, ds, bdq, bdg, regs):
        rows = (end - first) * CELLS
        dv = dot(p, bdg)
        dk = dot(ds, bdq)
        dv_s[a, first * CELLS : end * CELLS, :] += dv[:rows]
        dk_s[a, first * CELLS : end * CELLS, :] += dk[:rows]
        if regs:
            rv_s[...] += dv[rows:]
            rk_s[...] += dk[rows:]

    def diag_pair(q, g):
        bdq = block_diag(q.reshape(CELLS, 256) * jnp.asarray(SCALE, BF16))
        return bdq, block_diag(g.reshape(CELLS, 256))

    def local_q(a, block):
        return diag_pair(q_in[a, :, block], g_in[a, :, block])

    def local_keys(a, first, end):
        keys = jnp.concatenate([kb[a, first * CELLS : end * CELLS, :], reg_k], axis=0)
        values = jnp.concatenate([vb[a, first * CELLS : end * CELLS, :], reg_v], axis=0)
        return keys, values

    def local_stats(a, block, first, end):
        keys, values = local_keys(a, first, end)
        bdq, bdg = local_q(a, block)
        rep = mrep[a, first * CELLS : end * CELLS, :]
        add = jnp.concatenate(
            [bias(rep, first - block, off_ref[a, block]), jnp.zeros((2 * REG_DEV, 256), F32)], axis=0
        )
        e, dp, stats = partial_stats(keys, values, bdq, bdg, add)
        return keys, bdq, bdg, e, dp, stats

    def edge_stats(a, carry):
        for i, (block, first, end, side, _, _, _) in enumerate(EDGE):
            rows = (end - first) * CELLS + 2 * REG_DEV
            _, _, _, e, dp, stats = local_stats(a, block, first, end)
            e_s[a, i, :rows] = e
            p_s[a, i, :rows] = dp
            slot = i % 2
            for r in range(2):
                own_st[side, a, slot, r : r + 1] = stats[r]
            st_out[side, a, slot, 0:1] = stats[0] + jnp.log(stats[1])
            st_out[side, a, slot, 1:2] = probabilities(e, dp, 1.0 / stats[1])[2]
        return carry

    def middle(a, carry):
        keys, bdq, bdg, e, dp, stats = local_stats(a, 2, 0, NB)
        p, low, delta = probabilities(e, dp, 1.0 / stats[1])
        ds = score_grads(p, dp, delta)
        add_key_grads(a, 0, NB, low, ds, bdq, bdg, True)
        dq = diag_rows(dot(ds, keys, TN)) * SCALE
        o_q[a, :, 2] = dq.reshape(WIN, WIN, 256).astype(BF16)
        return carry

    def foreign_keys(side):
        mask_copy(1 - side).wait_recv()
        for kind in range(2):
            kv_copy(1 - side, kind).wait_recv()

        def body(a, carry):
            mask64 = mask_rows(fmask[side, pl.ds(pl.multiple_of(a * WIN, WIN), WIN), :])
            for slot in range(2):
                frep[slot * CELLS : (slot + 1) * CELLS, :] = mask_cells(mask64, slot + (3 if side == 0 else 0))
            for i, (block, first, end, edge_side, low, high, relative) in enumerate(EDGE):
                if edge_side != side:
                    continue
                rows = (end - first) * CELLS + 2 * REG_DEV
                far_k = jnp.concatenate(
                    [fk[side, a, :, slot].reshape(CELLS, 256) for slot in range(low, high)], axis=0
                )
                far_v = jnp.concatenate(
                    [fv[side, a, :, slot].reshape(CELLS, 256) for slot in range(low, high)], axis=0
                )
                keys, _ = local_keys(a, first, end)
                bdq, bdg = local_q(a, block)
                add = bias(frep[low * CELLS : high * CELLS, :], relative - block, off_ref[a, block])
                far_e, far_dp, far = partial_stats(far_k, far_v, bdq, bdg, add)
                near = tuple(own_st[side, a, i % 2, r : r + 1] for r in range(2))
                alpha, far_alpha = merged(near, far)
                dp = p_s[a, i, :rows]
                p, low_p, share = probabilities(e_s[a, i, :rows], dp, alpha)
                far_p, _, far_share = probabilities(far_e, far_dp, far_alpha)
                delta = share + far_share
                ds = score_grads(p, dp, delta)
                far_ds = score_grads(far_p, far_dp, delta)
                dq = diag_rows(dot(ds, keys, TN) + dot(far_ds, far_k, TN)) * SCALE
                add_key_grads(a, first, end, low_p, ds, bdq, bdg, True)
                o_q[a, :, block] = dq.reshape(WIN, WIN, 256).astype(BF16)
            return carry

        lax.fori_loop(0, NA, body, 0)

    def far_slot(side, blocks):
        return blocks - 1 + side * (3 - 2 * blocks)

    def row0_arrived(side):
        offset_copy(1 - side).wait_recv()
        st_copy(1 - side).wait_recv()
        for kind in range(2):
            qg_copy(1 - side, 0, kind).wait_recv()

    def row1_arrived(side, blocks):
        for kind in range(2):
            one_copy(1 - side, far_slot(side, blocks), kind).wait_recv()

    def far_bias(side, a, blocks):
        slot = far_slot(side, blocks)
        first = side * (NB - blocks)
        relative = jnp.where(side == 0, blocks - 3, 7 - blocks)
        cells = rows_of(first, blocks)
        here = (off_row == a) & (off_col == slot + 3 * (1 - side))
        start = jnp.sum(
            jnp.sum(jnp.where(here, far_off[side].astype(F32), 0.0), axis=1, keepdims=True),
            axis=0, keepdims=True,
        ).astype(jnp.int32)
        return bias(mrep[a, cells, :], first - relative, start)

    def far_weights(side, a, blocks, add=None):
        slot = far_slot(side, blocks)
        first = side * (NB - blocks)
        relative = jnp.where(side == 0, blocks - 3, 7 - blocks)
        cells = rows_of(first, blocks)
        bdq, bdg = diag_pair(fq[side, a, :, slot], fg[side, a, :, slot])
        top = st_in[side, a, slot, 0:1]
        theirs = (top, jnp.ones_like(top))
        if add is None:
            add = far_bias(side, a, blocks)
        e, dp, stats = partial_stats(kb[a, cells, :], vb[a, cells, :], bdq, bdg, add)
        alpha, their_alpha = merged(stats, theirs)
        p, low, share = probabilities(e, dp, alpha)
        ds = score_grads(p, dp, share + their_alpha * st_in[side, a, slot, 1:2])
        return cells, bdq, bdg, (low, ds)

    def add_far(a, unit):
        cells, bdq, bdg, (p, ds) = unit
        dv_s[a, cells, :] += dot(p, bdg)
        dk_s[a, cells, :] += dot(ds, bdq)

    def one_side(side, a):
        @pl.when(a == 0)
        def _():
            row0_arrived(side)

        for blocks in (2, 1):
            @pl.when(a == 1)
            def _():
                row1_arrived(side, blocks)

            add_far(a, far_weights(side, a, blocks))

    def both_sides(a):
        @pl.when(a == 0)
        def _():
            for side in range(2):
                row0_arrived(side)

        @pl.when(a == 1)
        def _():
            for side in range(2):
                for blocks in (2, 1):
                    row1_arrived(side, blocks)

        units = [far_weights(side, a, blocks) for blocks in (2, 1) for side in range(2)]
        for unit in units:
            add_far(a, unit)

    def spread(a, low, high):
        for b in range(low, high):
            mine = row8 == reg_ref[a, b]
            rep = mrep[a, b * CELLS : (b + 1) * CELLS, :]
            rep2 = jnp.concatenate([rep, rep], axis=1)
            for own, total, out in ((rrecv[0], dk_s, o_k), (rrecv[1], dv_s, o_v)):
                row = jnp.sum(jnp.where(mine, own, 0.0), axis=0, keepdims=True)
                cells = total[a, b * CELLS : (b + 1) * CELLS, :] + rep2 * row
                out[a, :, b] = cells.reshape(WIN, WIN, 256).astype(BF16)

    lax.fori_loop(0, NA, edge_stats, 0)
    for copy in later(1):
        copy.start()

    @pl.when(jnp.logical_not(first_tile))
    def _():
        for copy in later(0):
            copy.start()

    lax.fori_loop(0, NA, middle, 0)

    @pl.when(first_tile)
    def _():
        pl.semaphore_wait(late, 1)
        for copy in early(0) + later(0):
            copy.start()

    reg_copy = pltpu.make_async_remote_copy(
        rsend, rrecv, lat_ss.at[1], lat_rs.at[1], device_id={"lat": peer}, device_id_type=MESH
    )
    foreign_keys(1)

    def left_keys():
        foreign_keys(0)
        rsend[0] = rk_s[REG_DEV:, :]
        rsend[1] = rv_s[REG_DEV:, :]
        reg_copy.start()

    def registers_done():
        reg_copy.wait_recv()
        rrecv[0] = (rk_s[:REG_DEV, :] + rrecv[0]) / divisor
        rrecv[1] = (rv_s[:REG_DEV, :] + rrecv[1]) / divisor

    def step(i, carry):
        @pl.when(i == jnp.where(first_tile, 2, 0))
        def _():
            left_keys()

        @pl.when(first_tile & (i != 2))
        def _():
            one_side((i < 2).astype(jnp.int32), jnp.where(i < 2, i, i - 3))

        @pl.when(jnp.logical_not(first_tile) & (i > 0))
        def _():
            both_sides(i - 1)

        @pl.when(i == jnp.where(first_tile, 3, 1))
        def _():
            registers_done()
            spread(0, 0, NB)
            spread(1, 2, 3)

        @pl.when(i == jnp.where(first_tile, 3, 2))
        def _():
            spread(1, 3, NB)

        return carry

    lax.fori_loop(0, jnp.where(first_tile, 4, 3), step, 0)

    @pl.when(first_tile)
    def _():
        adds = {blocks: far_bias(0, 1, blocks) for blocks in (2, 1)}
        for blocks in (2, 1):
            row1_arrived(0, blocks)
        units = [far_weights(0, 1, blocks, adds[blocks]) for blocks in (2, 1)]
        for unit in units:
            add_far(1, unit)

    spread(1, 0, 2)
    for side in range(2):
        for copy in early(side) + later(side):
            copy.wait_send()
    pool_copy.wait_send()
    reg_copy.wait_send()


def store(a_in, b_in, c_in, a_out, b_out, c_out, sem):
    pairs = ((a_in, a_out), (b_in, b_out), (c_in, c_out))
    copies = [pltpu.make_async_copy(src, dst, sem.at[i]) for i, (src, dst) in enumerate(pairs)]
    for copy in copies:
        copy.start()
    for copy in copies:
        copy.wait()


def local(queries, keys, values, grad_out, key_mask, offsets, regions):
    shape = queries.shape
    grid = (NA, WIN, NB, WIN, 256)
    edge = (2, NA, WIN, 2, WIN, 256)
    hbm_spec = pl.BlockSpec(memory_space=pltpu.HBM)
    vm = pltpu.VMEM
    dma = pltpu.SemaphoreType.DMA
    outs = pl.pallas_call(
        kernel,
        out_shape=[pltpu.VMEM(grid, BF16)] * 3,
        in_specs=[hbm_spec] * 7,
        out_specs=[pl.BlockSpec(memory_space=pltpu.VMEM)] * 3,
        scratch_shapes=[vm(grid, BF16)] * 4
        + [vm((NA, NB * CELLS, 256), BF16)] * 2
        + [vm((NA, NB * CELLS, 128), F32), vm((2 * CELLS, 128), F32)]
        + [vm(edge, BF16)] * 4
        + [vm((2,) + key_mask.shape, jnp.int32)]
        + [vm((NA, 4, 4 * CELLS + 2 * REG_DEV, 256), F32)] * 2
        + [vm((NA, NB * CELLS, 256), F32)] * 2
        + [vm((2 * REG_DEV, 256), F32)] * 2
        + [vm((2, 2, REG_DEV, 256), BF16)]
        + [vm((2, REG_DEV, 256), F32)] * 2
        + [vm((2, NA, 2, 8, 256), F32)]
        + [vm((2, NA, 2, 2, 256), F32)] * 2
        + [vm((2,) + offsets.shape, jnp.int32)]
        + [vm(key_mask.shape, jnp.int32)]
        + [pltpu.SMEM(offsets.shape, jnp.int32)] * 2
        + [dma((7,))]
        + [dma((2, 2))] * 2
        + [dma((2, NA, 2))] * 2
        + [dma((2,))] * 6
        + [dma((2, 2, 2))] * 2
        + [dma((2,))] * 2
        + [pltpu.SemaphoreType.REGULAR] * 4,
        compiler_params=pltpu.CompilerParams(
            collective_id=0, has_side_effects=True, vmem_limit_bytes=VMEM_BYTES
        ),
        cost_estimate=pl.CostEstimate(flops=2200000000, bytes_accessed=2300000, transcendentals=860000),
    )(
        *(x.reshape(grid) for x in (queries, keys, values, grad_out)), key_mask, offsets, regions
    )
    outs = pl.pallas_call(
        store,
        out_shape=[jax.ShapeDtypeStruct(grid, BF16)] * 3,
        in_specs=[pl.BlockSpec(memory_space=pl.ANY)] * 3,
        out_specs=[hbm_spec] * 3,
        scratch_shapes=[dma((3,))],
        compiler_params=pltpu.CompilerParams(vmem_limit_bytes=1024 * 1024),
    )(*outs)
    return tuple(x.reshape(shape) for x in outs)


def solution(mesh):
    tile = P("lat", "lon", "head")
    cells = P("lat", "lon")
    return jax.shard_map(
        local, mesh=mesh, in_specs=(tile,) * 4 + (cells,) * 3, out_specs=(tile,) * 3, check_vma=False
    )
```
